128 devices in a mesh: gz: 32 (over y, z, core), gy: 4 (over x).
Axes of the slice: x: 4, y: 4, z: 4, core: 2. Of those that a mesh axis runs over, the one named last changes fastest.
Arguments:
- features: bfloat16 [1024, 64, 512], P(('gz', 'gy')), may hold values from -6 to 6
- occupancy: int32 [1024, 512], P(('gz', 'gy')), may hold values from 0 to 1, as said below
- neighbors: int32 [1024, 27], P(('gz', 'gy')), may hold values from -1 to 1023, as said below
- coarse_dest: int32 [1024], P(('gz', 'gy')), may hold values from -1 to 8191, as said below
- w_sub: bfloat16 [27, 64, 64], replicated, may hold values from -0.15625 to 0.15625
- w_down: bfloat16 [8, 128, 64], replicated, may hold values from -0.25 to 0.25
- coarse_grad: bfloat16 [1024, 128, 512], P(('gz', 'gy')), may hold values from -6 to 6
Outputs:
- coarse: bfloat16 [1024, 128, 512], P(('gz', 'gy'))
- feat_grad: bfloat16 [1024, 64, 512], P(('gz', 'gy'))
- w_sub_grad: float32 [27, 64, 64], replicated
- w_down_grad: float32 [8, 128, 64], replicated
The draws below stay inside these ranges and needn't reach their ends.
Inputs may be any that keep to these rules, and one draw needn't show every extreme that they name: `neighbors`: slot s of tile slot index t = d * 8 + s lies on device d = gz index * 4 + gy index. Tiles sit on a grid, each device's region being 2 x 4 x 8 tile positions; its active tiles fill slots 0 upward, the rest are -1 everywhere. An entry is another tile's slot only if that tile is the geometric neighbor, which lies on the same device or on a device whose gz index differs by the z displacement and whose gy index differs by the y displacement (never both by wrapping); the table is symmetric. Some device fills all 8 slots. `occupancy`: 0 on slots without a tile. `coarse_dest`: entries of tiles are distinct; the coarse tile c lies on device c // 8, which is the slot's own device or the one whose gz index differs only in its lowest bit, with the same gy index.
All inputs are finite; a program needn't handle non-finite values.
Results may differ from the reference program's by a relative error of at most 0.005.
The reference program's roundings to bfloat16 on the way (of `masked`, `padded`, `activated`, `blocks`, `out_grad`, `act_grad` and `pre_grad`) count: a program that leaves them out, or rounds other values in their place, can miss the bound.
Values may be sent and summed in bfloat16 or wider, within the bound.
A program may use at most 192 MiB of HBM per device.

```python
import jax
import jax.numpy as jnp
from jax import lax

CH = 64
CO = 128
TD = 8
RZ = 2
RY = 4
RX = 8
SLABS = 32
STRIPS = 4
TILES = 1024
CD = 8
CTILES = 1024


def tile_layout(key):
    devices_all = SLABS * STRIPS
    places = RZ * RY * RX
    keys_all = jax.random.split(jax.random.fold_in(key, 101), devices_all)
    ranking = jax.vmap(lambda part_key: jax.random.permutation(part_key, places))(keys_all)
    last_row = ranking[devices_all - 1]
    last_value = last_row[places - 1]
    last_row = jnp.where(last_row == 0, last_value, last_row).at[places - 1].set(0)
    ranking = ranking.at[devices_all - 1].set(last_row)
    tile_counts = jax.random.randint(jax.random.fold_in(key, 102), (devices_all,), TD // 2, TD + 1)
    tile_counts = tile_counts.at[0].set(TD).at[devices_all - 1].set(TD)
    chosen = ranking < tile_counts[:, None]
    slot_of = jnp.cumsum(chosen.astype(jnp.int32), axis=1) - 1
    device_ids = jnp.arange(devices_all, dtype=jnp.int32)[:, None]
    tile_ids = jnp.where(chosen, device_ids * TD + slot_of, -1).astype(jnp.int32)
    target = jnp.where(chosen, slot_of, TD)
    place_ids = jnp.broadcast_to(jnp.arange(places, dtype=jnp.int32)[None, :], (devices_all, places))
    row_ids = jnp.broadcast_to(device_ids, (devices_all, places))
    where_slot = jnp.full((devices_all, TD), -1, jnp.int32).at[row_ids, target].set(place_ids, mode='drop')
    return (tile_ids, where_slot)


def coordinates(where_slot):
    devices_all = SLABS * STRIPS
    device_ids = jnp.broadcast_to(jnp.arange(devices_all, dtype=jnp.int32)[:, None], (devices_all, TD))
    local_z = where_slot // (RY * RX)
    local_y = where_slot // RX % RY
    local_x = where_slot % RX
    fine_z = device_ids // STRIPS * RZ + local_z
    fine_y = device_ids % STRIPS * RY + local_y
    present = where_slot >= 0
    return (fine_z.reshape(-1), fine_y.reshape(-1), local_x.reshape(-1), present.reshape(-1))


def draw_neighbors(key, part):
    tile_ids, where_slot = tile_layout(key)
    grid = tile_ids.reshape(SLABS, STRIPS, RZ, RY, RX).transpose(0, 2, 1, 3, 4)
    grid = grid.reshape(SLABS * RZ, STRIPS * RY, RX)
    grid = jnp.pad(grid, 1, constant_values=-1)
    fine_z, fine_y, fine_x, present = coordinates(where_slot)
    fine_z = jnp.maximum(fine_z, 0)
    fine_y = jnp.maximum(fine_y, 0)
    fine_x = jnp.maximum(fine_x, 0)
    columns = []
    for a in range(3):
        for b in range(3):
            for c in range(3):
                columns.append(grid[fine_z + a, fine_y + b, fine_x + c])
    table = jnp.stack(columns, axis=1)
    return jnp.where(present[:, None], table, -1).astype(jnp.int32)


def draw_occupancy(key, part):
    tile_ids, where_slot = tile_layout(key)
    key = jax.random.fold_in(key, 8)
    fine_z, fine_y, fine_x, present = coordinates(where_slot)
    levels = jax.random.randint(jax.random.fold_in(key, 1), (TILES, 1), 15, 96)
    rolls = jax.random.randint(jax.random.fold_in(key, 2), (TILES, 512), 0, 100)
    return jnp.where(present[:, None] & (rolls < levels), 1, 0).astype(jnp.int32)


def draw_coarse_dest(key, part):
    tile_ids, where_slot = tile_layout(key)
    fine_z, fine_y, fine_x, present = coordinates(where_slot)
    half_x = RX // 4
    half_y = RY // 2
    coarse_z = fine_z // 2
    coarse_y = fine_y // 2
    coarse_x = fine_x // 2
    owner_z = 2 * (coarse_z // 2) + coarse_x // half_x
    owner = owner_z * STRIPS + coarse_y // half_y
    coarse_slot = (coarse_z % 2 * half_y + coarse_y % half_y) * half_x + coarse_x % half_x
    octant = fine_z % 2 * 4 + fine_y % 2 * 2 + fine_x % 2
    return jnp.where(present, (owner * CD + coarse_slot) * 8 + octant, -1).astype(jnp.int32)


def block_levels(stream_key, extent, pieces, smallest, largest):
    loudness, own = 1.0, jax.random.fold_in(stream_key, 6)
    for dim, shards_of in pieces:
        heights = jnp.exp(jax.random.uniform(jax.random.fold_in(own, dim), (shards_of,), jnp.float32, smallest / len(pieces), largest / len(pieces)))
        loudness = loudness * jnp.repeat(heights, extent[dim] // shards_of).reshape([-1 if axis == dim else 1 for axis in range(len(extent))])
    return loudness


def normal_values(rng, shape, scale, most, cuts=(), kind=jnp.bfloat16):
    values = jax.random.normal(rng, shape, jnp.float32) * scale
    if len(cuts) > 0:
        values = block_levels(rng, shape, cuts, -0.22, 0.18) * values
    return jnp.clip(values, min=-most, max=most).astype(kind)


def setup_inputs(seed: int = 0) -> dict:
    key_of = jax.random.split(jax.random.key(seed), 8)
    features = normal_values(key_of[0], (TILES, CH, 512), 1.0, 6.0, ((0, 128),))
    occupancy = draw_occupancy(jax.random.fold_in(key_of[7], 71), 0)
    neighbors = draw_neighbors(jax.random.fold_in(key_of[7], 71), 0)
    coarse_dest = draw_coarse_dest(jax.random.fold_in(key_of[7], 71), 0)
    w_sub = normal_values(key_of[4], (27, CH, CH), (27 * CH) ** -0.5, 0.15625)
    w_down = normal_values(key_of[5], (8, CO, CH), (8 * CH) ** -0.5, 0.25)
    coarse_grad = normal_values(key_of[6], (CTILES, CO, 512), 1.0, 6.0, ((0, 128),))
    return dict(features=features, occupancy=occupancy, neighbors=neighbors, coarse_dest=coarse_dest, w_sub=w_sub, w_down=w_down, coarse_grad=coarse_grad)


def rim_ranges(index):
    if index == 0:
        return slice(7, 8), slice(0, 1)
    if index == 1:
        return slice(0, 8), slice(1, 9)
    return slice(0, 1), slice(9, 10)


def pad_block(field5, links):
    rows = links.shape[0]
    padded = jnp.zeros((rows, field5.shape[1], 10, 10, 10), field5.dtype)
    for a in range(3):
        for b in range(3):
            for c in range(3):
                from_z, into_z = rim_ranges(a)
                from_y, into_y = rim_ranges(b)
                from_x, into_x = rim_ranges(c)
                target = links[:, 9 * a + 3 * b + c]
                portion = field5[jnp.maximum(target, 0)][:, :, from_z, from_y, from_x]
                portion = jnp.where((target >= 0)[:, None, None, None, None], portion, jnp.zeros_like(portion))
                padded = padded.at[:, :, into_z, into_y, into_x].set(portion)
    return padded


def conv_sum(padded, w_sub, flipped):
    rows, channels = padded.shape[0], padded.shape[1]
    weights = w_sub.astype(jnp.float32)
    total = jnp.zeros((rows, channels, 512), jnp.float32)
    for a in range(3):
        for b in range(3):
            for c in range(3):
                start_z, start_y, start_x = (2 - a, 2 - b, 2 - c) if flipped else (a, b, c)
                window = padded[:, :, start_z:start_z + 8, start_y:start_y + 8, start_x:start_x + 8]
                window = window.reshape(rows, channels, 512).astype(jnp.float32)
                if flipped:
                    total = total + jnp.einsum('oi,tov->tiv', weights[9 * a + 3 * b + c], window)
                else:
                    total = total + jnp.einsum('oi,tiv->tov', weights[9 * a + 3 * b + c], window)
    return total


def split_phases(field):
    rows, channels = field.shape[0], field.shape[1]
    field = field.reshape(rows, channels, 4, 2, 4, 2, 4, 2).transpose(0, 3, 5, 7, 1, 2, 4, 6)
    return field.reshape(rows, 8, channels, 64)


def merge_phases(field):
    rows, channels = field.shape[0], field.shape[2]
    field = field.reshape(rows, 2, 2, 2, channels, 4, 4, 4).transpose(0, 4, 5, 1, 6, 2, 7, 3)
    return field.reshape(rows, channels, 512)


def assemble(flat):
    tiles_now = flat.shape[0] // 8
    outer = flat.reshape(tiles_now, 2, 2, 2, flat.shape[1], 4, 4, 4).transpose(0, 4, 1, 5, 2, 6, 3, 7)
    return outer.reshape(tiles_now, flat.shape[1], 512)


def disassemble(field):
    tiles_now = field.shape[0]
    inner = field.reshape(tiles_now, field.shape[1], 2, 4, 2, 4, 2, 4).transpose(0, 2, 4, 6, 1, 3, 5, 7)
    return inner.reshape(tiles_now * 8, field.shape[1], 64)


def reference(features, occupancy, neighbors, coarse_dest, w_sub, w_down, coarse_grad):
    devices_all = SLABS * STRIPS
    occupied = occupancy.astype(jnp.float32)[:, None, :]
    masked = features * occupancy.astype(jnp.bfloat16)[:, None, :]
    masked5 = masked.reshape(TILES, CH, 8, 8, 8)
    links_all = neighbors.reshape(devices_all, TD, 27)
    occ_all = occupied.reshape(devices_all, TD, 1, 512)

    def forward_block(inputs):
        links, occ_here = inputs
        preact = conv_sum(pad_block(masked5, links), w_sub, False)
        activated = (jax.nn.silu(preact) * occ_here).astype(jnp.bfloat16)
        return preact, activated

    preact, activated = lax.map(forward_block, (links_all, occ_all))
    preact = preact.reshape(TILES, CH, 512)
    activated = activated.reshape(TILES, CH, 512)
    phases = split_phases(activated).astype(jnp.float32)
    down = w_down.astype(jnp.float32)
    blocks = jnp.einsum('koi,tkiv->tov', down, phases).astype(jnp.bfloat16)
    index = jnp.where(coarse_dest >= 0, coarse_dest, CTILES * 8)
    flat = jnp.zeros((CTILES * 8, CO, 64), jnp.bfloat16).at[index].set(blocks, mode="drop")
    coarse = assemble(flat)

    grad_flat = disassemble(coarse_grad)
    out_grad = grad_flat[jnp.maximum(coarse_dest, 0)]
    out_grad = jnp.where((coarse_dest >= 0)[:, None, None], out_grad, jnp.zeros_like(out_grad))
    out_grad32 = out_grad.astype(jnp.float32)
    act_grad = merge_phases(jnp.einsum('koi,tov->tkiv', down, out_grad32)).astype(jnp.bfloat16)
    w_down_sum = jnp.einsum('tov,tkiv->koi', out_grad32, phases)
    sigma = jax.nn.sigmoid(preact)
    pre_grad = (act_grad.astype(jnp.float32) * sigma * (1.0 + preact * (1.0 - sigma)) * occupied).astype(jnp.bfloat16)
    pre_grad5 = pre_grad.reshape(TILES, CH, 8, 8, 8)
    grad_all = pre_grad.reshape(devices_all, TD, CH, 512)

    def backward_block(inputs):
        links, occ_here, own_grad = inputs
        feat_grad = (conv_sum(pad_block(pre_grad5, links), w_sub, True) * occ_here).astype(jnp.bfloat16)
        x_padded = pad_block(masked5, links)
        own32 = own_grad.astype(jnp.float32)
        terms = []
        for a in range(3):
            for b in range(3):
                for c in range(3):
                    window = x_padded[:, :, a:a + 8, b:b + 8, c:c + 8].reshape(TD, CH, 512).astype(jnp.float32)
                    terms.append(jnp.einsum('tov,tiv->oi', own32, window))
        return feat_grad, jnp.stack(terms)

    feat_grad, w_parts = lax.map(backward_block, (links_all, occ_all, grad_all))
    scale = (TILES * 512.0) ** -0.5
    w_sub_grad = jnp.sum(w_parts, axis=0) * scale
    return coarse, feat_grad.reshape(TILES, CH, 512), w_sub_grad, w_down_sum * scale
```

```python
import functools

import jax
import jax.numpy as jnp
import numpy as np
from jax import lax
from jax.experimental import pallas as pl
from jax.experimental.pallas import tpu as pltpu
from jax.sharding import PartitionSpec as P

MESH = pl.DeviceIdType.MESH
BF = jnp.bfloat16
F32 = jnp.float32

Y_LOW, Y_HIGH, ZERO, Z_LOW, Z_HIGH, DIAGONAL, BANK = 64, 128, 192, 200, 208, 216, 248


def one_hot(shape, pairs):
    out = np.zeros(shape, np.float32)
    for row, column in pairs:
        out[row, column] = 1.0
    return jnp.asarray(out, BF)


def lane(y, x):
    return 10 * (y + 1) + x + 1


def permutations():
    wrap = [
        (64 * h + 8 * ((yp - 1) % 8) + (xp - 1) % 8, 128 * h + 10 * yp + xp)
        for h in range(2) for yp in range(10) for xp in range(10)
    ]
    rewrap = [
        (lane((yp - 1) % 8, (xp - 1) % 8), 10 * yp + xp) for yp in range(10) for xp in range(10)
    ]
    native = [
        (128 * h + lane(y, x), 64 * h + 8 * y + x)
        for h in range(2) for y in range(8) for x in range(8)
    ]
    pack = [
        (128 * z + 10 * (0 if side == 0 else 9) + xp, 128 * side + 10 * z + xp)
        for side in range(2) for z in range(8) for xp in range(10)
    ]
    unpack = [
        [(10 * z + xp, 128 * z + 90 * side + xp) for z in range(8) for xp in range(10)]
        for side in range(2)
    ]
    phase, octant = [], []
    for z in range(8):
        for y in range(8):
            for x in range(8):
                k = 4 * (z % 2) + 2 * (y % 2) + x % 2
                v = 16 * (z // 2) + 4 * (y // 2) + x // 2
                phase.append((128 * z + lane(y, x), 64 * k + v))
                k = 4 * (z // 4) + 2 * (y // 4) + x // 4
                v = 16 * (z % 4) + 4 * (y % 4) + x % 4
                octant.append((64 * k + v, 64 * z + 8 * y + x))
    flip = lambda pairs: [(b, a) for a, b in pairs]
    return (
        one_hot((128, 256), wrap),
        one_hot((128, 128), rewrap),
        one_hot((256, 128), native),
        one_hot((1024, 256), pack),
        one_hot((128, 1024), unpack[0]),
        one_hot((128, 1024), unpack[1]),
        one_hot((1024, 512), phase),
        one_hot((512, 1024), flip(phase)),
        one_hot((512, 512), octant),
        one_hot((512, 512), flip(octant)),
    )


def dot(a, b):
    return jnp.dot(a, b, preferred_element_type=F32)


def dot_nt(a, b):
    return lax.dot_general(a, b, (((1,), (1,)), ((), ())), preferred_element_type=F32)


def roll(x, shift):
    return pltpu.roll(x, shift % 128, x.ndim - 1)


def body(
    scale,
    feat, occ, nbr, dest_v, dest_s, w_sub, w_down, cgrad,
    p_wrap, p_rewrap, p_native, p_pack, p_un0, p_un1, p_phase, p_unphase, p_oct, p_unoct,
    coarse, feat_grad, ws_out, wd_out,
    bank1, bank2, ysend, ydst, zsend, dsend, drecv, idx_v, idx_s, inv_v, inv_s, dest_buf, dest_in,
    cg_bank, og_in, og_all, og, ag_ph, ag, occ_p, r_buf, act, phases, pg, wf, wb, wd, wdt,
    bl, bl_in, bl_bank, fg, wg, ws_src, ws_ra, ws_red, ws_rb, ws_gb, ws_ga,
    wd_src, wd_ra, wd_red, wd_rb, wd_gb, wd_ga,
    h_send, h_recv, c_send, c_recv, idx_sem, r_send, r_recv,
):
    gz, gy = lax.axis_index("gz"), lax.axis_index("gy")
    cy, cz, core = gz // 8, (gz // 2) % 4, gz % 2
    nz, ny = 32, 4

    def at(dz, dy):
        return {"gz": (gz + dz + nz) % nz, "gy": (gy + dy + ny) % ny}

    partner = {"gz": gz + 1 - 2 * core, "gy": gy}
    halo_steps = [(dz, dy) for dz in (-1, 0, 1) for dy in (-1, 0, 1) if (dz, dy) != (0, 0)]
    a_steps = [(dc, dx) for dx in range(4) for dc in range(2) if (dc, dx) != (0, 0)]
    b_steps = [(dy, dz) for dy in range(4) for dz in range(4) if (dy, dz) != (0, 0)]

    def a_peer(dc, dx):
        return {"gz": gz - core + (core + dc) % 2, "gy": (gy + dx) % 4}

    def b_peer(dy, dz):
        return {"gz": ((cy + dy) % 4 * 4 + (cz + dz) % 4) * 2 + core, "gy": gy}

    barrier = pltpu.get_barrier_semaphore()
    for device in (
        [at(*s) for s in halo_steps] + [a_peer(*s) for s in a_steps] + [b_peer(*s) for s in b_steps]
    ):
        pl.semaphore_signal(barrier, inc=1, device_id=device, device_id_type=MESH)

    def send(src, dst, send_sem, recv_sem, device):
        copy = pltpu.make_async_remote_copy(
            src_ref=src, dst_ref=dst, send_sem=send_sem, recv_sem=recv_sem,
            device_id=device, device_id_type=MESH,
        )
        copy.start()
        return copy

    lanes = lax.broadcasted_iota(jnp.int32, (64, 128), 1)
    low_half = lax.broadcasted_iota(jnp.int32, (128, 128), 1) < 64
    xp = lanes - 10 * lax.shift_right_logical(lanes * 205, 11)
    first, last = xp == 0, xp == 9
    yp_low, yp_high = lanes < 10, lanes >= 90
    center_row = lax.broadcasted_iota(jnp.int32, (8, 128), 1)
    center_x = center_row - 10 * lax.shift_right_logical(center_row * 205, 11)
    center = (center_row > 10) & (center_row < 89) & (center_x > 0) & (center_x < 9)

    table = nbr[...]
    owner = table // 8
    slot = table - owner * 8
    step_z = owner // 4 - gz
    step_y = owner - owner // 4 * 4 - gy
    column = lax.broadcasted_iota(jnp.int32, (8, 27), 1)
    part_a = column // 9
    edge_z = jnp.where(part_a == 0, 7, 0)
    on_z = Z_LOW + jnp.where(step_z > 0, 8, 0) + slot
    on_diagonal = DIAGONAL + jnp.where(step_z > 0, 16, 0) + jnp.where(step_y > 0, 8, 0) + slot
    same_z = jnp.where(step_y == 0, 0, jnp.where(step_y < 0, Y_LOW, Y_HIGH)) + slot * 8 + edge_z
    index = jnp.where(step_z == 0, same_z, jnp.where(step_y == 0, on_z, on_diagonal))
    index = jnp.where((table < 0) | ((part_a == 1) & (index > ZERO)), ZERO, index)
    idx_v[...] = jnp.zeros_like(idx_v)
    idx_v[:, 0:27] = index
    idx_copy = pltpu.make_async_copy(idx_v, idx_s, idx_sem.at[0])
    idx_copy.start()

    for q in range(4):
        part = feat[:, :, 128 * q:128 * q + 128]
        flag = occ[:, 128 * q:128 * q + 128].astype(F32).astype(BF)
        rows = [part[t] * flag[t:t + 1] for t in range(8)]
        planes = dot(jnp.concatenate(rows, axis=0), p_wrap[...]).astype(BF)
        flags = dot(flag, p_wrap[...])
        for h in range(2):
            flag_plane = jnp.where(center, flags[:, 128 * h:128 * h + 128], 0.0)
            for t in range(8):
                occ_p[t, :, 128 * (2 * q + h):128 * (2 * q + h) + 128] = flag_plane[t:t + 1]
                bank1[8 * t + 2 * q + h] = planes[64 * t:64 * t + 64, 128 * h:128 * h + 128]

    dest_buf[0] = jnp.zeros((8, 128), jnp.int32) - 1
    dest_buf[0, 0:1, 0:8] = dest_v[...]
    for bank in (bank1, bank2):
        bank[ZERO:ZERO + 8] = jnp.zeros((8, 64, 128), BF)

    pl.semaphore_wait(barrier, len(halo_steps) + len(a_steps) + len(b_steps))

    dest_send = send(dest_buf.at[0], dest_buf.at[1], c_send.at[0], c_recv.at[0], partner)
    cg_send = send(cgrad, cg_bank.at[pl.ds(8, 8)], c_send.at[1], c_recv.at[1], partner)
    local_cg = pltpu.make_async_copy(cgrad, cg_bank.at[pl.ds(0, 8)], idx_sem.at[1])
    local_cg.start()

    def publish(bank, which):
        copies = []
        total = None
        for q in range(4):
            both = jnp.concatenate(
                [
                    jnp.concatenate([bank[8 * t + 2 * q], bank[8 * t + 2 * q + 1]], axis=1)
                    for t in range(8)
                ],
                axis=0,
            )
            term = dot(both, p_pack[256 * q:256 * q + 256, :])
            total = term if total is None else total + term
        rows = total.astype(BF)
        for side in range(2):
            for t in range(8):
                ysend[which, side, t] = rows[64 * t:64 * t + 64, 128 * side:128 * side + 128]
                zsend[which, side, t] = bank[8 * t + (7 if side == 0 else 0)]
        for side in range(2):
            up = 1 - 2 * side
            copies.append(
                send(
                    ysend.at[which, side], ydst.at[which, side],
                    h_send.at[which, side], h_recv.at[which, side], at(0, up),
                )
            )
            copies.append(
                send(
                    zsend.at[which, side], bank.at[pl.ds(Z_LOW if side == 0 else Z_HIGH, 8)],
                    h_send.at[which, 2 + side], h_recv.at[which, 2 + side], at(up, 0),
                )
            )
        for side_z in range(2):
            for side_y in range(2):
                number = 2 * side_z + side_y
                gathered = None
                for t in range(8):
                    piece = total[64 * t:64 * t + 64, 128 * side_y:128 * side_y + 128]
                    piece = roll(piece, 16 * t - (70 if side_z == 0 else 0))
                    piece = jnp.where((lanes >= 16 * t) & (lanes < 16 * t + 10), piece, 0.0)
                    gathered = piece if gathered is None else gathered + piece
                dsend[which, number] = gathered.astype(BF)
                copies.append(
                    send(
                        dsend.at[which, number], drecv.at[which, number],
                        h_send.at[which, 4 + number], h_recv.at[which, 4 + number],
                        at(1 - 2 * side_z, 1 - 2 * side_y),
                    )
                )
        return copies

    def receive(bank, which, copies):
        for copy in copies:
            copy.wait_recv()
        for side in range(2):
            rows = ydst[which, side].reshape(512, 128)
            for q in range(4):
                planes = dot(rows, (p_un0, p_un1)[side][:, 256 * q:256 * q + 256]).astype(BF)
                for t in range(8):
                    for h in range(2):
                        bank[(Y_LOW, Y_HIGH)[side] + 8 * t + 2 * q + h] = planes[
                            64 * t:64 * t + 64, 128 * h:128 * h + 128
                        ]
        for side_z in range(2):
            for side_y in range(2):
                number = 2 * side_z + side_y
                packed = drecv[which, number].astype(F32)
                for t in range(8):
                    bank[DIAGONAL + 8 * number + t] = roll(packed, 90 * side_y - 16 * t).astype(BF)

    def assemble(bank, t):
        masks = {0: (yp_low,), 1: (), 2: (yp_high,)}
        for zp in range(10):
            a = 0 if zp == 0 else (2 if zp == 9 else 1)
            rows = []
            for b in range(3):
                loaded = []
                for c in range(3):
                    place = idx_s[t, 9 * a + 3 * b + c] + (zp - 1 if a == 1 else 0)
                    loaded.append(bank[place])
                rows.append(jnp.where(first, loaded[0], jnp.where(last, loaded[2], loaded[1])))
            plane = jnp.where(yp_low, rows[0], jnp.where(yp_high, rows[2], rows[1]))
            wide = plane.astype(F32)
            columns = slice(128 * zp, 128 * zp + 128)
            r_buf[t, 0:64, columns] = roll(wide, 10).astype(BF)
            r_buf[t, 64:128, columns] = plane
            r_buf[t, 128:192, columns] = roll(wide, -10).astype(BF)

    def convolve(weights, t, q):
        total = None
        for a in range(3):
            term = dot(weights[a], r_buf[t, :, 128 * a + 256 * q:128 * a + 256 * q + 256])
            total = term if total is None else total + term
        parts = []
        for h in range(2):
            y = total[:, 128 * h:128 * h + 128]
            parts.append(roll(y[0:64], 1) + y[64:128] + roll(y[128:192], -1))
        return parts

    halo = publish(bank1, 0)

    for a in range(3):
        for c in range(3):
            wf[a, 64 * c:64 * c + 64, :] = jnp.concatenate(
                [w_sub[9 * a + 3 * b + c].astype(F32) for b in range(3)], axis=1
            ).astype(BF)
        turned = jnp.concatenate(
            [
                jnp.concatenate(
                    [w_sub[9 * (2 - a) + 3 * (2 - b) + 2 - c].astype(F32) for c in range(3)], axis=1
                )
                for b in range(3)
            ],
            axis=0,
        )
        wb[a] = turned.T.astype(BF)
    wide = jnp.concatenate([w_down[k].astype(F32) for k in range(8)], axis=1)
    wd[...] = wide.astype(BF)
    wdt[...] = wide.T.astype(BF)

    cg_bank[16] = jnp.zeros((128, 512), BF)
    idx_copy.wait()
    local_cg.wait()
    cg_send.wait_recv()
    base = gz * 4 + gy
    partner_index = (gz + 1 - 2 * core) * 4 + gy
    for t in range(8):
        d = dest_s[0, t]
        own = d // 8 - base * 8
        other = d // 8 - partner_index * 8
        chosen = jnp.where((other >= 0) & (other < 8), 8 + other, 16)
        chosen = jnp.where((own >= 0) & (own < 8), own, chosen)
        og_in[128 * t:128 * t + 128, :] = cg_bank[chosen]
    for q in range(2):
        split = dot(og_in[...], p_unoct[:, 256 * q:256 * q + 256]).astype(BF)
        for t in range(8):
            for h in range(2):
                og_all[4 * t + 2 * q + h] = split[128 * t:128 * t + 128, 128 * h:128 * h + 128]
    for j in range(4):
        halves = []
        for h in range(2):
            t = 2 * j + h
            d = dest_s[0, t]
            octant = d - d // 8 * 8
            piece = og_all[4 * t + octant // 2].astype(F32)
            odd = octant - octant // 2 * 2
            halves.append(jnp.where(odd == h, piece, roll(piece, 64)))
        og[:, 128 * j:128 * j + 128] = jnp.where(low_half, halves[0], halves[1]).astype(BF)
    low64 = lanes < 64
    for r in range(4):
        rows = dot(wdt[128 * r:128 * r + 128, :], og[...]).astype(BF).astype(F32)
        for j in range(4):
            even = rows[0:64, 128 * j:128 * j + 128]
            odd = rows[64:128, 128 * j:128 * j + 128]
            columns = slice(128 * r, 128 * r + 128)
            ag_ph[128 * j:128 * j + 64, columns] = jnp.where(low64, even, roll(odd, 64)).astype(BF)
            ag_ph[128 * j + 64:128 * j + 128, columns] = jnp.where(
                low64, roll(even, 64), odd
            ).astype(BF)
    for q in range(4):
        spread = dot(ag_ph[...], p_unphase[:, 256 * q:256 * q + 256]).astype(BF)
        for t in range(8):
            ag[t, :, 256 * q:256 * q + 256] = spread[64 * t:64 * t + 64]

    dest_send.wait_recv()
    dest_copy = pltpu.make_async_copy(dest_buf.at[1], dest_in, idx_sem.at[2])
    dest_copy.start()
    dest_copy.wait()
    place = lax.broadcasted_iota(jnp.int32, (8, 128), 1) + base * 64
    inverse = jnp.zeros((8, 128), jnp.int32) + 16
    for s in range(8):
        inverse = jnp.where(place == dest_s[0, s], s, inverse)
        inverse = jnp.where(place == dest_in[0, s], 8 + s, inverse)
    inv_v[...] = inverse
    inv_copy = pltpu.make_async_copy(inv_v, inv_s, idx_sem.at[3])
    inv_copy.start()

    receive(bank1, 0, halo)

    @pl.loop(0, 8)
    def _(t):
        assemble(bank1, t)
        for q in range(4):
            parts = convolve(wf, t, q)
            for h in range(2):
                z = 2 * q + h
                v = parts[h]
                on = occ_p[t, :, 128 * z:128 * z + 128]
                s = 1.0 / (1.0 + jnp.exp(-v))
                act[t, :, 128 * z:128 * z + 128] = jnp.where(on > 0.5, v * s, 0.0).astype(BF)
                g = ag[t, :, 128 * z:128 * z + 128].astype(F32)
                g = g * s * (1.0 + v * (1.0 - s))
                pg[8 * t + z] = jnp.where(on > 0.5, g, 0.0).astype(BF)

    @pl.loop(0, 8)
    def _(t):
        rows = pg[pl.ds(8 * t, 8)].reshape(512, 128)
        bank2[pl.ds(8 * t, 8)] = dot(rows, p_rewrap[...]).astype(BF).reshape(8, 64, 128)

    halo2 = publish(bank2, 1)

    for q in range(2):
        split = dot(act[...].reshape(512, 1024), p_phase[:, 256 * q:256 * q + 256])
        for j in range(4):
            for h in range(2):
                even = split[128 * j:128 * j + 64, 128 * h:128 * h + 128]
                odd = split[128 * j + 64:128 * j + 128, 128 * h:128 * h + 128]
                k = 4 * q + 2 * h
                columns = slice(128 * j, 128 * j + 128)
                phases[64 * k:64 * k + 64, columns] = jnp.where(
                    low64, even, roll(odd, 64)
                ).astype(BF)
                phases[64 * k + 64:64 * k + 128, columns] = jnp.where(
                    low64, roll(even, 64), odd
                ).astype(BF)
    bl[...] = dot(wd[...], phases[...]).astype(BF)
    bl_send = send(bl, bl_in, c_send.at[2], c_recv.at[2], partner)
    down = dot_nt(og[...], phases[...])
    for k in range(8):
        half = down[:, 128 * (k // 2):128 * (k // 2) + 128]
        half = half if k % 2 == 0 else roll(half, 64)
        wd_src[128 * k:128 * k + 128, :] = jnp.where(low_half, half, 0.0)

    def reducer(which, src, ra, red, rb, gb, ga):
        me_a, me_b = gy * 2 + core, cy * 4 + cz
        rows_a = pl.ds(pl.multiple_of(me_a * 128, 128), 128)
        rows_b = pl.ds(pl.multiple_of(me_b * 8, 8), 8)
        sems = lambda n: (r_send.at[which, n], r_recv.at[which, n])

        def start_a():
            copies = []
            for n, (dc, dx) in enumerate(a_steps):
                m = (gy + dx) % 4 * 2 + (core + dc) % 2
                rows = src.at[pl.ds(pl.multiple_of(m * 128, 128), 128)]
                copies.append(send(rows, ra.at[n], *sems(n), a_peer(dc, dx)))
            return copies

        def finish_a(copies):
            for copy in copies:
                copy.wait_recv()
            total = src[rows_a]
            for n in range(7):
                total = total + ra[n]
            red[...] = total

        def start_b():
            copies = []
            for n, (dy, dz) in enumerate(b_steps):
                j = (cy + dy) % 4 * 4 + (cz + dz) % 4
                rows = red.at[pl.ds(pl.multiple_of(j * 8, 8), 8)]
                copies.append(send(rows, rb.at[n], *sems(7 + n), b_peer(dy, dz)))
            return copies

        def finish_b(copies):
            for copy in copies:
                copy.wait_recv()
            total = red[rows_b]
            for n in range(15):
                total = total + rb[n]
            gb[rows_b] = total * scale

        def start_gb():
            return [
                send(gb.at[rows_b], gb.at[rows_b], *sems(22 + n), b_peer(dy, dz))
                for n, (dy, dz) in enumerate(b_steps)
            ]

        def finish_gb(copies):
            for copy in copies:
                copy.wait_recv()
            ga[rows_a] = gb[...]

        def start_ga():
            return [
                send(gb, ga.at[rows_a], *sems(37 + n), a_peer(dc, dx))
                for n, (dc, dx) in enumerate(a_steps)
            ]

        def finish_ga(copies):
            for copy in copies:
                copy.wait_recv()

        started = []
        starts, finishes = (start_a, start_b, start_gb, start_ga), (
            finish_a, finish_b, finish_gb, finish_ga
        )

        def step():
            n = len(started)
            if n > 0:
                finishes[n - 1](started[n - 1])
            if n < 4:
                started.append(starts[n]())

        def drain():
            for copies in started:
                for copy in copies:
                    copy.wait_send()

        return step, drain

    down_step, down_drain = reducer(1, wd_src, wd_ra, wd_red, wd_rb, wd_gb, wd_ga)
    sub_step, sub_drain = reducer(0, ws_src, ws_ra, ws_red, ws_rb, ws_gb, ws_ga)
    down_step()

    wg[...] = jnp.zeros_like(wg)

    @pl.loop(0, 8)
    def _(t):
        planes = [pg[8 * t + z].astype(F32) for z in range(8)]
        shifted = jnp.concatenate(
            [
                jnp.concatenate([roll(p, c - 1).astype(BF) for p in planes], axis=1)
                for c in range(3)
            ],
            axis=0,
        )
        for a in range(3):
            wg[a] += dot_nt(shifted, r_buf[t, :, 128 * a:128 * a + 1024])

    for a in range(3):
        ws_src[192 * a:192 * a + 192, :] = wg[a, :, 0:128]
    ws_src[576:768, :] = jnp.concatenate([wg[0, :, 128:192], wg[1, :, 128:192]], axis=1)
    ws_src[768:960, 0:64] = wg[2, :, 128:192]
    ws_src[768:960, 64:128] = jnp.zeros((192, 64), F32)
    ws_src[960:1024, :] = jnp.zeros((64, 128), F32)
    sub_step()

    receive(bank2, 1, halo2)
    down_step()

    def backward(low, high):
        @pl.loop(low, high)
        def _(t):
            assemble(bank2, t)
            for q in range(4):
                parts = convolve(wb, t, q)
                for h in range(2):
                    z = 2 * q + h
                    on = occ_p[t, :, 128 * z:128 * z + 128]
                    fg[t, :, 128 * z:128 * z + 128] = jnp.where(on > 0.5, parts[h], 0.0).astype(BF)

    backward(0, 3)
    sub_step()
    down_step()
    backward(3, 6)
    sub_step()
    down_step()
    backward(6, 8)
    for q in range(4):
        rows = dot(fg[:, :, 256 * q:256 * q + 256].reshape(512, 256), p_native[...])
        feat_grad[:, :, 128 * q:128 * q + 128] = rows.astype(BF).reshape(8, 64, 128)
    sub_step()
    down_step()

    inv_copy.wait()
    bl_send.wait_recv()
    bl_bank[16] = jnp.zeros((128, 128), BF)
    for source in range(2):
        blocks = (bl, bl_in)[source]
        for j in range(4):
            pair = blocks[:, 128 * j:128 * j + 128].astype(F32)
            turned = roll(pair, 64)
            bl_bank[8 * source + 2 * j] = jnp.where(low_half, pair, turned).astype(BF)
            bl_bank[8 * source + 2 * j + 1] = jnp.where(low_half, turned, pair).astype(BF)
    for c in range(8):
        for q in range(4):
            even = bl_bank[inv_s[0, 8 * c + 2 * q]]
            odd = bl_bank[inv_s[0, 8 * c + 2 * q + 1]]
            og_in[128 * c:128 * c + 128, 128 * q:128 * q + 128] = jnp.where(low_half, even, odd)
    for q in range(2):
        rows = dot(og_in[...], p_oct[:, 256 * q:256 * q + 256]).astype(BF)
        coarse[:, :, 256 * q:256 * q + 256] = rows.reshape(8, 128, 256)

    sub_step()
    for a in range(3):
        for c in range(3):
            for b in range(2):
                rows = slice(192 * a + 64 * c, 192 * a + 64 * c + 64)
                ws_out[9 * a + 3 * b + c] = ws_ga[rows, 64 * b:64 * b + 64]
            row, column = ((576, 0), (576, 64), (768, 0))[a]
            rows = slice(row + 64 * c, row + 64 * c + 64)
            ws_out[9 * a + 6 + c] = ws_ga[rows, column:column + 64]
    for k in range(8):
        wd_out[k] = wd_ga[128 * k:128 * k + 128, 0:64]
    for copy in halo + halo2 + [dest_send, cg_send, bl_send]:
        copy.wait_send()
    sub_drain()
    down_drain()


def shards(features, occupancy, neighbors, coarse_dest, w_sub, w_down, coarse_grad):
    devices = lax.axis_size("gz") * lax.axis_size("gy")
    scale = (features.shape[0] * devices * 512.0) ** -0.5
    dest = coarse_dest.reshape(1, 8)
    vmem, anywhere = pl.BlockSpec(memory_space=pltpu.VMEM), pl.BlockSpec(memory_space=pl.ANY)
    in_specs = [vmem, vmem, vmem, vmem, pl.BlockSpec(memory_space=pltpu.SMEM), vmem, vmem, anywhere]
    in_specs += [vmem] * 10
    reducing = [
        pltpu.VMEM((1024, 128), F32),
        pltpu.VMEM((7, 128, 128), F32),
        pltpu.VMEM((128, 128), F32),
        pltpu.VMEM((15, 8, 128), F32),
        pltpu.VMEM((128, 128), F32),
        pltpu.VMEM((1024, 128), F32),
    ]
    return pl.pallas_call(
        functools.partial(body, scale),
        out_shape=(
            jax.ShapeDtypeStruct((8, 128, 512), BF),
            jax.ShapeDtypeStruct((8, 64, 512), BF),
            jax.ShapeDtypeStruct((27, 64, 64), F32),
            jax.ShapeDtypeStruct((8, 128, 64), F32),
        ),
        in_specs=in_specs,
        out_specs=(vmem,) * 4,
        scratch_shapes=[
            pltpu.VMEM((BANK, 64, 128), BF),
            pltpu.VMEM((BANK, 64, 128), BF),
            pltpu.VMEM((2, 2, 8, 64, 128), BF),
            pltpu.VMEM((2, 2, 8, 64, 128), BF),
            pltpu.VMEM((2, 2, 8, 64, 128), BF),
            pltpu.VMEM((2, 4, 64, 128), BF),
            pltpu.VMEM((2, 4, 64, 128), BF),
            pltpu.VMEM((8, 128), jnp.int32),
            pltpu.SMEM((8, 128), jnp.int32),
            pltpu.VMEM((8, 128), jnp.int32),
            pltpu.SMEM((8, 128), jnp.int32),
            pltpu.VMEM((2, 8, 128), jnp.int32),
            pltpu.SMEM((8, 128), jnp.int32),
            pltpu.VMEM((17, 128, 512), BF),
            pltpu.VMEM((1024, 512), BF),
            pltpu.VMEM((32, 128, 128), BF),
            pltpu.VMEM((128, 512), BF),
            pltpu.VMEM((512, 512), BF),
            pltpu.VMEM((8, 64, 1024), BF),
            pltpu.VMEM((8, 1, 1024), F32),
            pltpu.VMEM((8, 192, 1280), BF),
            pltpu.VMEM((8, 64, 1024), BF),
            pltpu.VMEM((512, 512), BF),
            pltpu.VMEM((64, 64, 128), BF),
            pltpu.VMEM((3, 192, 192), BF),
            pltpu.VMEM((3, 192, 192), BF),
            pltpu.VMEM((128, 512), BF),
            pltpu.VMEM((512, 128), BF),
            pltpu.VMEM((128, 512), BF),
            pltpu.VMEM((128, 512), BF),
            pltpu.VMEM((17, 128, 128), BF),
            pltpu.VMEM((8, 64, 1024), BF),
            pltpu.VMEM((3, 192, 192), F32),
        ] + reducing + reducing + [
            pltpu.SemaphoreType.DMA((2, 8)),
            pltpu.SemaphoreType.DMA((2, 8)),
            pltpu.SemaphoreType.DMA((3,)),
            pltpu.SemaphoreType.DMA((3,)),
            pltpu.SemaphoreType.DMA((4,)),
            pltpu.SemaphoreType.DMA((2, 44)),
            pltpu.SemaphoreType.DMA((2, 44)),
        ],
        compiler_params=pltpu.CompilerParams(
            collective_id=0, has_side_effects=True, vmem_limit_bytes=60 * 1024 * 1024
        ),
        cost_estimate=pl.CostEstimate(flops=6 * 10**9, bytes_accessed=12 * 10**6, transcendentals=10**6),
        name="sparse_conv",
    )(features, occupancy, neighbors, dest, dest, w_sub, w_down, coarse_grad, *permutations())


def solution(mesh):
    return jax.shard_map(
        shards,
        mesh=mesh,
        in_specs=(
            P(("gz", "gy"), None, None),
            P(("gz", "gy"), None),
            P(("gz", "gy"), None),
            P(("gz", "gy")),
            P(),
            P(),
            P(("gz", "gy"), None, None),
        ),
        out_specs=(P(("gz", "gy"), None, None), P(("gz", "gy"), None, None), P(), P()),
        check_vma=False,
    )
```

```python
import functools

import jax
import jax.numpy as jnp
import numpy as np
from jax import lax
from jax.experimental import pallas as pl
from jax.experimental.pallas import tpu as pltpu
from jax.sharding import PartitionSpec as P

MESH = pl.DeviceIdType.MESH
BF = jnp.bfloat16
F32 = jnp.float32

Y_LOW, Y_HIGH, ZERO, Z_LOW, Z_HIGH, DIAGONAL, BANK = 64, 128, 192, 200, 208, 216, 248


def one_hot(shape, pairs):
    out = np.zeros(shape, np.float32)
    for row, column in pairs:
        out[row, column] = 1.0
    return jnp.asarray(out, BF)


def lane(y, x):
    return 10 * (y + 1) + x + 1


def permutations():
    wrap = [
        (64 * h + 8 * ((yp - 1) % 8) + (xp - 1) % 8, 128 * h + 10 * yp + xp)
        for h in range(2) for yp in range(10) for xp in range(10)
    ]
    rewrap = [
        (lane((yp - 1) % 8, (xp - 1) % 8), 10 * yp + xp) for yp in range(10) for xp in range(10)
    ]
    native = [
        (128 * h + lane(y, x), 64 * h + 8 * y + x)
        for h in range(2) for y in range(8) for x in range(8)
    ]
    pack = [
        (128 * z + 90 * side + x + 1, 64 * side + 8 * z + x)
        for side in range(2) for z in range(8) for x in range(8)
    ]
    unpack = [
        [
            (64 * parity + 8 * z + (xp - 1) % 8, 1024 * parity + 128 * z + 90 * side + xp)
            for parity in range(2) for z in range(8) for xp in range(10)
        ]
        for side in range(2)
    ]
    phase, octant = [], []
    for z in range(8):
        for y in range(8):
            for x in range(8):
                k = 4 * (z % 2) + 2 * (y % 2) + x % 2
                v = 16 * (z // 2) + 4 * (y // 2) + x // 2
                phase.append((128 * z + lane(y, x), 64 * k + v))
                k = 4 * (z // 4) + 2 * (y // 4) + x // 4
                v = 16 * (z % 4) + 4 * (y % 4) + x % 4
                octant.append((64 * k + v, 64 * z + 8 * y + x))
    flip = lambda pairs: [(b, a) for a, b in pairs]
    return (
        one_hot((128, 256), wrap),
        one_hot((128, 128), rewrap),
        one_hot((256, 128), native),
        one_hot((1024, 128), pack),
        one_hot((128, 2048), unpack[0]),
        one_hot((128, 2048), unpack[1]),
        one_hot((1024, 512), phase),
        one_hot((512, 1024), flip(phase)),
        one_hot((512, 512), octant),
        one_hot((512, 512), flip(octant)),
    )


def dot(a, b):
    return jnp.dot(a, b, preferred_element_type=F32)


def dot_nt(a, b):
    return lax.dot_general(a, b, (((1,), (1,)), ((), ())), preferred_element_type=F32)


def roll(x, shift):
    return pltpu.roll(x, shift % 128, x.ndim - 1)


PERMUTATIONS = ("wrap", "rewrap", "native", "pack", "un0", "un1", "phase", "unphase", "oct", "unoct")


def body(scale, *refs):
    operands, results, scratch = refs[:17], refs[17:21], refs[21:]
    nbr_h, occ_h, feat_h, dest_h, w_sub_h, w_down_h, cgrad = operands[:7]
    coarse, feat_grad, ws_out, wd_out = results
    nbr, occ, feat, dest_v, dest_s, w_sub, w_down = scratch[:7]
    p_wrap, p_rewrap, p_native, p_pack, p_un0, p_un1, p_phase, p_unphase, p_oct, p_unoct = scratch[7:17]
    (
        bank1, bank2, ysend, ydst, zsend, dsend, drecv, idx_v, idx_s, inv_v, inv_s, dest_buf, dest_in,
        cg_bank, og_in, og_all, og, ag_ph, ag, occ_p, r0, r1, act, phases, pg, wf, wb, wd, wdt,
        bl, bl_in, bl_bank, fg, wg, coarse_v, feat_v, ws_v,
        src, rc, s1, t1, t2, t3, fin, wd_v,
        h_send, h_recv, c_send, c_recv, in_sem, idx_sem, out_sem, r_send, r_recv,
    ) = scratch[17:]
    gz, gy = lax.axis_index("gz"), lax.axis_index("gy")
    cy, cz, core = gz // 8, (gz // 2) % 4, gz % 2
    nz, ny = 32, 4

    def at(dz, dy):
        return {"gz": (gz + dz + nz) % nz, "gy": (gy + dy + ny) % ny}

    def along(axis, d):
        if axis == 0:
            return {"gz": gz, "gy": (gy + d) % 4}
        if axis == 1:
            return {"gz": ((cy + d) % 4 * 4 + cz) * 2 + core, "gy": gy}
        return {"gz": (cy * 4 + (cz + d) % 4) * 2 + core, "gy": gy}

    coordinate = (gy, cy, cz)
    partner = {"gz": gz + 1 - 2 * core, "gy": gy}
    halo_steps = [(dz, dy) for dz in (-1, 0, 1) for dy in (-1, 0, 1) if (dz, dy) != (0, 0)]
    barrier = pltpu.get_barrier_semaphore()
    greeted = [at(*s) for s in halo_steps] + [partner]
    greeted += [along(axis, d) for axis in range(3) for d in (1, 2, 3)]
    for device in greeted:
        pl.semaphore_signal(barrier, inc=1, device_id=device, device_id_type=MESH)

    loads = {}

    def load(name, source, target):
        loads[name] = pltpu.make_async_copy(source, target, in_sem.at[len(loads)])
        loads[name].start()

    permuting = dict(zip(PERMUTATIONS, zip(operands[7:], scratch[7:17])))
    load("feat", feat_h, feat)
    load("occ", occ_h, occ)
    load("wrap", *permuting["wrap"])
    load("nbr", nbr_h, nbr)
    load("dest", dest_h, dest_v)
    load("dest_s", dest_h, dest_s)
    load("pack", *permuting["pack"])
    load("w_sub", w_sub_h, w_sub)
    load("w_down", w_down_h, w_down)
    load("cgrad", cgrad, cg_bank.at[pl.ds(0, 8)])
    for name in ("unoct", "unphase", "un0", "un1", "rewrap", "phase", "native", "oct"):
        load(name, *permuting[name])

    def send(src, dst, send_sem, recv_sem, device):
        copy = pltpu.make_async_remote_copy(
            src_ref=src, dst_ref=dst, send_sem=send_sem, recv_sem=recv_sem,
            device_id=device, device_id_type=MESH,
        )
        copy.start()
        return copy

    lanes = lax.broadcasted_iota(jnp.int32, (64, 128), 1)
    low_half = lax.broadcasted_iota(jnp.int32, (128, 128), 1) < 64
    xp = lanes - 10 * lax.shift_right_logical(lanes * 205, 11)
    first, last = xp == 0, xp == 9
    low64 = lanes < 64
    yp_low, yp_high = lanes < 10, lanes >= 90
    center_row = lax.broadcasted_iota(jnp.int32, (8, 128), 1)
    center_x = center_row - 10 * lax.shift_right_logical(center_row * 205, 11)
    center = (center_row > 10) & (center_row < 89) & (center_x > 0) & (center_x < 9)

    loads["nbr"].wait()
    table = nbr[...]
    owner = table // 8
    slot = table - owner * 8
    step_z = owner // 4 - gz
    step_y = owner - owner // 4 * 4 - gy
    column = lax.broadcasted_iota(jnp.int32, (8, 27), 1)
    part_a = column // 9
    edge_z = jnp.where(part_a == 0, 7, 0)
    on_z = Z_LOW + jnp.where(step_z > 0, 8, 0) + slot
    on_diagonal = DIAGONAL + jnp.where(step_z > 0, 16, 0) + jnp.where(step_y > 0, 8, 0) + slot
    same_z = jnp.where(step_y == 0, 0, jnp.where(step_y < 0, Y_LOW, Y_HIGH)) + slot * 8 + edge_z
    index = jnp.where(step_z == 0, same_z, jnp.where(step_y == 0, on_z, on_diagonal))
    index = jnp.where((table < 0) | ((part_a == 1) & (index > ZERO)), ZERO, index)
    idx_v[...] = jnp.zeros_like(idx_v)
    idx_v[:, 0:27] = index
    idx_copy = pltpu.make_async_copy(idx_v, idx_s, idx_sem.at[0])
    idx_copy.start()

    loads["feat"].wait()
    loads["occ"].wait()
    loads["wrap"].wait()
    for q in range(4):
        part = feat[:, :, 128 * q:128 * q + 128]
        flag = occ[:, 128 * q:128 * q + 128].astype(F32).astype(BF)
        rows = [part[t] * flag[t:t + 1] for t in range(8)]
        planes = dot(jnp.concatenate(rows, axis=0), p_wrap[...]).astype(BF)
        flags = dot(flag, p_wrap[...])
        for h in range(2):
            flag_plane = jnp.where(center, flags[:, 128 * h:128 * h + 128], 0.0)
            for t in range(8):
                occ_p[t, :, 128 * (2 * q + h):128 * (2 * q + h) + 128] = flag_plane[t:t + 1]
                bank1[8 * t + 2 * q + h] = planes[64 * t:64 * t + 64, 128 * h:128 * h + 128]

    loads["dest"].wait()
    dest_buf[0] = jnp.zeros((8, 128), jnp.int32) - 1
    dest_buf[0, 0:1, 0:8] = dest_v[...]
    for bank in (bank1, bank2):
        bank[ZERO:ZERO + 8] = jnp.zeros((8, 64, 128), BF)
    loads["pack"].wait()

    pl.semaphore_wait(barrier, len(greeted))
    dest_send = send(dest_buf.at[0], dest_buf.at[1], c_send.at[0], c_recv.at[0], partner)
    cg_send = send(cgrad, cg_bank.at[pl.ds(8, 8)], c_send.at[1], c_recv.at[1], partner)

    def publish(bank, which):
        copies = []
        total = None
        for q in range(4):
            both = jnp.concatenate(
                [
                    jnp.concatenate([bank[8 * t + 2 * q], bank[8 * t + 2 * q + 1]], axis=1)
                    for t in range(8)
                ],
                axis=0,
            )
            term = dot(both, p_pack[256 * q:256 * q + 256, :])
            total = term if total is None else total + term
        for j in range(4):
            even, odd = total[128 * j:128 * j + 64], total[128 * j + 64:128 * j + 128]
            ysend[which, 0, j] = jnp.where(low64, even, roll(odd, 64)).astype(BF)
            ysend[which, 1, j] = jnp.where(low64, roll(even, 64), odd).astype(BF)
        for side in range(2):
            for t in range(8):
                zsend[which, side, t] = bank[8 * t + (7 if side == 0 else 0)]
        for side in range(2):
            up = 1 - 2 * side
            copies.append(
                send(
                    ysend.at[which, side], ydst.at[which, side],
                    h_send.at[which, side], h_recv.at[which, side], at(0, up),
                )
            )
            copies.append(
                send(
                    zsend.at[which, side], bank.at[pl.ds(Z_LOW if side == 0 else Z_HIGH, 8)],
                    h_send.at[which, 2 + side], h_recv.at[which, 2 + side], at(up, 0),
                )
            )
        for side_z in range(2):
            for side_y in range(2):
                number = 2 * side_z + side_y
                gathered = None
                for t in range(8):
                    piece = bank[8 * t + (7 if side_z == 0 else 0)].astype(F32)
                    piece = roll(piece, 16 * t - 90 * side_y)
                    piece = jnp.where((lanes >= 16 * t) & (lanes < 16 * t + 10), piece, 0.0)
                    gathered = piece if gathered is None else gathered + piece
                dsend[which, number] = gathered.astype(BF)
                copies.append(
                    send(
                        dsend.at[which, number], drecv.at[which, number],
                        h_send.at[which, 4 + number], h_recv.at[which, 4 + number],
                        at(1 - 2 * side_z, 1 - 2 * side_y),
                    )
                )
        return copies

    def receive(bank, which, copies):
        for copy in copies:
            copy.wait_recv()
        for side in range(2):
            rows = ydst[which, side].reshape(256, 128)
            for q in range(8):
                planes = dot(rows, (p_un0, p_un1)[side][:, 256 * q:256 * q + 256]).astype(BF)
                for j in range(4):
                    for h in range(2):
                        t, z = 2 * j + q // 4, 2 * (q % 4) + h
                        bank[(Y_LOW, Y_HIGH)[side] + 8 * t + z] = planes[
                            64 * j:64 * j + 64, 128 * h:128 * h + 128
                        ]
        for side_z in range(2):
            for side_y in range(2):
                number = 2 * side_z + side_y
                packed = drecv[which, number].astype(F32)
                for t in range(8):
                    bank[DIAGONAL + 8 * number + t] = roll(packed, 90 * side_y - 16 * t).astype(BF)

    def assemble(bank, t, r_buf, i, planes):
        for zp in planes:
            a = 0 if zp == 0 else (2 if zp == 9 else 1)
            rows = []
            for b in range(3):
                loaded = []
                for c in range(3):
                    place = idx_s[t, 9 * a + 3 * b + c] + (zp - 1 if a == 1 else 0)
                    loaded.append(bank[place])
                rows.append(jnp.where(first, loaded[0], jnp.where(last, loaded[2], loaded[1])))
            plane = jnp.where(yp_low, rows[0], jnp.where(yp_high, rows[2], rows[1]))
            wide = plane.astype(F32)
            columns = slice(128 * zp, 128 * zp + 128)
            r_buf[i, 0:64, columns] = roll(wide, 10).astype(BF)
            r_buf[i, 64:128, columns] = plane
            r_buf[i, 128:192, columns] = roll(wide, -10).astype(BF)

    def convolve(weights, r_buf, i, q):
        total = None
        for a in range(3):
            term = dot(weights[a], r_buf[i, :, 128 * a + 256 * q:128 * a + 256 * q + 256])
            total = term if total is None else total + term
        parts = []
        for h in range(2):
            y = total[:, 128 * h:128 * h + 128]
            parts.append(roll(y[0:64], 1) + y[64:128] + roll(y[128:192], -1))
        return parts

    groups = ((0, 1, 2), (3, 4, 5), (6, 7), (8, 9))

    def sweep(bank, low, high, tile):
        if low == 0:
            for planes in groups:
                assemble(bank, 0, r0, 0, planes)

        @pl.loop(low, high)
        def _(i):
            for q in range(4):
                assemble(bank, 2 * i + 1, r1, i, groups[q])
                tile(r0, i, 2 * i, q)
            for q in range(4):
                assemble(bank, jnp.minimum(2 * i + 2, 7), r0, i + 1, groups[q])
                tile(r1, i, 2 * i + 1, q)

    halo = publish(bank1, 0)

    loads["w_sub"].wait()
    loads["w_down"].wait()
    for a in range(3):
        for c in range(3):
            wf[a, 64 * c:64 * c + 64, :] = jnp.concatenate(
                [w_sub[9 * a + 3 * b + c].astype(F32) for b in range(3)], axis=1
            ).astype(BF)
        turned = jnp.concatenate(
            [
                jnp.concatenate(
                    [w_sub[9 * (2 - a) + 3 * (2 - b) + 2 - c].astype(F32) for c in range(3)], axis=1
                )
                for b in range(3)
            ],
            axis=0,
        )
        wb[a] = turned.T.astype(BF)
    wdt[...] = w_down[...].reshape(512, 128)
    wd[...] = wdt[...].astype(F32).T.astype(BF)

    cg_bank[16] = jnp.zeros((128, 512), BF)
    idx_copy.wait()
    loads["dest_s"].wait()
    loads["cgrad"].wait()
    loads["unoct"].wait()
    cg_send.wait_recv()
    base = gz * 4 + gy
    partner_index = (gz + 1 - 2 * core) * 4 + gy
    for t in range(8):
        d = dest_s[0, t]
        own = d // 8 - base * 8
        other = d // 8 - partner_index * 8
        chosen = jnp.where((other >= 0) & (other < 8), 8 + other, 16)
        chosen = jnp.where((own >= 0) & (own < 8), own, chosen)
        og_in[128 * t:128 * t + 128, :] = cg_bank[chosen]
    for q in range(2):
        split = dot(og_in[...], p_unoct[:, 256 * q:256 * q + 256]).astype(BF)
        for t in range(8):
            for h in range(2):
                og_all[4 * t + 2 * q + h] = split[128 * t:128 * t + 128, 128 * h:128 * h + 128]
    for j in range(4):
        halves = []
        for h in range(2):
            t = 2 * j + h
            d = dest_s[0, t]
            octant = d - d // 8 * 8
            piece = og_all[4 * t + octant // 2].astype(F32)
            odd = octant - octant // 2 * 2
            halves.append(jnp.where(odd == h, piece, roll(piece, 64)))
        og[:, 128 * j:128 * j + 128] = jnp.where(low_half, halves[0], halves[1]).astype(BF)
    for r in range(4):
        rows = dot(wdt[128 * r:128 * r + 128, :], og[...]).astype(BF).astype(F32)
        for j in range(4):
            even = rows[0:64, 128 * j:128 * j + 128]
            odd = rows[64:128, 128 * j:128 * j + 128]
            columns = slice(128 * r, 128 * r + 128)
            ag_ph[128 * j:128 * j + 64, columns] = jnp.where(low64, even, roll(odd, 64)).astype(BF)
            ag_ph[128 * j + 64:128 * j + 128, columns] = jnp.where(
                low64, roll(even, 64), odd
            ).astype(BF)
    loads["unphase"].wait()
    for q in range(4):
        spread = dot(ag_ph[...], p_unphase[:, 256 * q:256 * q + 256]).astype(BF)
        for t in range(8):
            ag[t, :, 256 * q:256 * q + 256] = spread[64 * t:64 * t + 64]

    dest_send.wait_recv()
    dest_copy = pltpu.make_async_copy(dest_buf.at[1], dest_in, idx_sem.at[2])
    dest_copy.start()
    dest_copy.wait()
    place = lax.broadcasted_iota(jnp.int32, (8, 128), 1) + base * 64
    inverse = jnp.zeros((8, 128), jnp.int32) + 16
    for s in range(8):
        inverse = jnp.where(place == dest_s[0, s], s, inverse)
        inverse = jnp.where(place == dest_in[0, s], 8 + s, inverse)
    inv_v[...] = inverse
    inv_copy = pltpu.make_async_copy(inv_v, inv_s, idx_sem.at[3])
    inv_copy.start()

    loads["un0"].wait()
    loads["un1"].wait()
    receive(bank1, 0, halo)

    def forward(r_buf, i, t, q):
        parts = convolve(wf, r_buf, i, q)
        for h in range(2):
            z = 2 * q + h
            v = parts[h]
            on = occ_p[t, :, 128 * z:128 * z + 128]
            s = 1.0 / (1.0 + jnp.exp(-v))
            act[t, :, 128 * z:128 * z + 128] = jnp.where(on > 0.5, v * s, 0.0).astype(BF)
            g = ag[t, :, 128 * z:128 * z + 128].astype(F32)
            g = g * s * (1.0 + v * (1.0 - s))
            pg[8 * t + z] = jnp.where(on > 0.5, g, 0.0).astype(BF)

    sweep(bank1, 0, 4, forward)

    wg[...] = jnp.zeros_like(wg)

    @pl.loop(0, 4)
    def _(i):
        for h in range(2):
            planes = [pg[8 * (2 * i + h) + z].astype(F32) for z in range(8)]
            shifted = jnp.concatenate(
                [
                    jnp.concatenate([roll(p, c - 1).astype(BF) for p in planes], axis=1)
                    for c in range(3)
                ],
                axis=0,
            )
            for a in range(3):
                wg[a] += dot_nt(shifted, (r0, r1)[h][i, :, 128 * a:128 * a + 1024])

    for a in range(3):
        src[192 * a:192 * a + 192, :] = wg[a, :, 0:128]
    src[576:768, :] = jnp.concatenate([wg[0, :, 128:192], wg[1, :, 128:192]], axis=1)
    src[768:960, 0:64] = wg[2, :, 128:192]
    src[768:960, 64:128] = jnp.zeros((192, 64), F32)

    loads["phase"].wait()
    for q in range(2):
        split = dot(act[...].reshape(512, 1024), p_phase[:, 256 * q:256 * q + 256])
        for j in range(4):
            for h in range(2):
                even = split[128 * j:128 * j + 64, 128 * h:128 * h + 128]
                odd = split[128 * j + 64:128 * j + 128, 128 * h:128 * h + 128]
                k = 4 * q + 2 * h
                columns = slice(128 * j, 128 * j + 128)
                phases[64 * k:64 * k + 64, columns] = jnp.where(
                    low64, even, roll(odd, 64)
                ).astype(BF)
                phases[64 * k + 64:64 * k + 128, columns] = jnp.where(
                    low64, roll(even, 64), odd
                ).astype(BF)
    src[960:1472, :] = dot_nt(phases[...], og[...])
    src[1472:1536, :] = jnp.zeros((64, 128), F32)

    reduced = []

    def pair(n):
        return r_send.at[n], r_recv.at[n]

    def rows_at(start, size):
        return pl.ds(pl.multiple_of(start, 8), size)

    def axis_of(p, stage):
        return (p + stage) % 3

    def me(p, stage):
        return coordinate[axis_of(p, stage)]

    def stage_0():
        return [
            [send(src.at[rows_at(768 * (1 - core) + 256 * p, 256)], rc.at[p], *pair(p), partner)]
            for p in range(3)
        ]

    def arrived(copies):
        for copy in copies:
            copy.wait_recv()

    def stage_1(before):
        out = []
        for p in range(3):
            arrived(before[p])
            s1[p] = src[rows_at(768 * core + 256 * p, 256)] + rc[p]
            copies = []
            for d in (1, 2, 3):
                to = (me(p, 0) + d) % 4
                copies.append(
                    send(
                        s1.at[p, rows_at(64 * to, 64)], t1.at[p, d - 1],
                        *pair(3 + 3 * p + d - 1), along(axis_of(p, 0), d),
                    )
                )
            out.append(copies)
        return out

    def stage_2(before):
        out = []
        for p in range(3):
            arrived(before[p])
            total = s1[p, rows_at(64 * me(p, 0), 64)]
            for d in range(3):
                total = total + t1[p, d]
            out.append(exchange(t2, p, 1, total, 12))
        return out

    def exchange(buffer, p, stage, value, first_pair):
        buffer[p, me(p, stage)] = value
        place = buffer.at[p, me(p, stage)]
        return [
            send(place, place, *pair(first_pair + 3 * p + d - 1), along(axis_of(p, stage), d))
            for d in (1, 2, 3)
        ]

    def stage_3(before):
        out = []
        for p in range(3):
            arrived(before[p])
            total = (t2[p, 0] + t2[p, 1]) + (t2[p, 2] + t2[p, 3])
            out.append(exchange(t3, p, 2, total, 21))
        return out

    def stage_4(before):
        out = []
        for p in range(3):
            arrived(before[p])
            rows = rows_at(768 * core + 256 * p + 64 * me(p, 0), 64)
            total = (t3[p, 0] + t3[p, 1]) + (t3[p, 2] + t3[p, 3])
            fin[rows] = (total * scale).astype(BF)
            out.append(
                [
                    send(fin.at[rows], fin.at[rows], *pair(30 + 3 * p + d - 1), along(axis_of(p, 0), d))
                    for d in (1, 2, 3)
                ]
            )
        return out

    def stage_5(before):
        out = []
        for p in range(3):
            arrived(before[p])
            rows = rows_at(768 * core + 256 * p, 256)
            out.append([send(fin.at[rows], fin.at[rows], *pair(39 + p), partner)])
        return out

    stages = [stage_0, stage_1, stage_2, stage_3, stage_4, stage_5]

    def reduce_step():
        n = len(reduced)
        reduced.append(stages[n](reduced[-1]) if n > 0 else stages[0]())

    reduce_step()

    loads["rewrap"].wait()
    for t in range(8):
        rows = pg[8 * t:8 * t + 8].reshape(512, 128)
        bank2[8 * t:8 * t + 8] = dot(rows, p_rewrap[...]).astype(BF).reshape(8, 64, 128)

    halo2 = publish(bank2, 1)

    bl[...] = dot(wd[...], phases[...]).astype(BF)
    bl_send = send(bl, bl_in, c_send.at[2], c_recv.at[2], partner)
    reduce_step()
    inv_copy.wait()
    bl_send.wait_recv()
    bl_bank[16] = jnp.zeros((128, 128), BF)
    for source in range(2):
        blocks = (bl, bl_in)[source]
        for j in range(4):
            both = blocks[:, 128 * j:128 * j + 128].astype(F32)
            turned = roll(both, 64)
            bl_bank[8 * source + 2 * j] = jnp.where(low_half, both, turned).astype(BF)
            bl_bank[8 * source + 2 * j + 1] = jnp.where(low_half, turned, both).astype(BF)
    for c in range(8):
        for q in range(4):
            even = bl_bank[inv_s[0, 8 * c + 2 * q]]
            odd = bl_bank[inv_s[0, 8 * c + 2 * q + 1]]
            og_in[128 * c:128 * c + 128, 128 * q:128 * q + 128] = jnp.where(low_half, even, odd)
    loads["oct"].wait()
    for q in range(2):
        rows = dot(og_in[...], p_oct[:, 256 * q:256 * q + 256]).astype(BF)
        coarse_v[:, :, 256 * q:256 * q + 256] = rows.reshape(8, 128, 256)
    coarse_out = pltpu.make_async_copy(coarse_v, coarse, out_sem.at[1])
    coarse_out.start()
    reduce_step()
    reduce_step()
    receive(bank2, 1, halo2)

    def backward(r_buf, i, t, q):
        parts = convolve(wb, r_buf, i, q)
        for h in range(2):
            z = 2 * q + h
            on = occ_p[t, :, 128 * z:128 * z + 128]
            fg[t, :, 128 * z:128 * z + 128] = jnp.where(on > 0.5, parts[h], 0.0).astype(BF)

    sweep(bank2, 0, 2, backward)
    reduce_step()
    sweep(bank2, 2, 4, backward)
    reduce_step()
    loads["native"].wait()
    for q in range(4):
        rows = dot(fg[:, :, 256 * q:256 * q + 256].reshape(512, 256), p_native[...])
        feat_v[:, :, 128 * q:128 * q + 128] = rows.astype(BF).reshape(8, 64, 128)
    feat_out = pltpu.make_async_copy(feat_v, feat_grad, out_sem.at[0])
    feat_out.start()

    for p in range(3):
        arrived(reduced[5][p])
    wd_v[...] = fin[960:1472, :].astype(F32)
    down_out = pltpu.make_async_copy(wd_v, wd_out, out_sem.at[2])
    down_out.start()
    for a in range(3):
        for c in range(3):
            for b in range(2):
                rows = slice(192 * a + 64 * c, 192 * a + 64 * c + 64)
                ws_v[9 * a + 3 * b + c] = fin[rows, 64 * b:64 * b + 64].astype(F32)
            row, column = ((576, 0), (576, 64), (768, 0))[a]
            rows = slice(row + 64 * c, row + 64 * c + 64)
            ws_v[9 * a + 6 + c] = fin[rows, column:column + 64].astype(F32)
    sub_out = pltpu.make_async_copy(ws_v, ws_out, out_sem.at[3])
    sub_out.start()
    for copy in halo + halo2 + [dest_send, cg_send, bl_send]:
        copy.wait_send()
    for stage in reduced:
        for copies in stage:
            for copy in copies:
                copy.wait_send()
    for copy in (feat_out, coarse_out, down_out, sub_out):
        copy.wait()


def shards(features, occupancy, neighbors, coarse_dest, w_sub, w_down, coarse_grad):
    devices = lax.axis_size("gz") * lax.axis_size("gy")
    scale = (features.shape[0] * devices * 512.0) ** -0.5
    anywhere = pl.BlockSpec(memory_space=pl.ANY)
    constants = permutations()
    vmem, smem, dma = pltpu.VMEM, pltpu.SMEM, pltpu.SemaphoreType.DMA
    i32 = jnp.int32
    coarse, feat_grad, ws, wd = pl.pallas_call(
        functools.partial(body, scale),
        out_shape=(
            vmem((8, 128, 512), BF), vmem((8, 64, 512), BF), vmem((27, 64, 64), F32), vmem((512, 128), F32),
        ),
        in_specs=[anywhere] * 17,
        out_specs=(anywhere,) * 4,
        scratch_shapes=[
            vmem((8, 27), i32), vmem((8, 512), i32), vmem((8, 64, 512), BF), vmem((1, 8), i32),
            smem((1, 8), i32), vmem((27, 64, 64), BF), vmem((8, 64, 128), BF),
        ] + [vmem(c.shape, BF) for c in constants] + [
            vmem((BANK, 64, 128), BF), vmem((BANK, 64, 128), BF),
            vmem((2, 2, 4, 64, 128), BF), vmem((2, 2, 4, 64, 128), BF), vmem((2, 2, 8, 64, 128), BF),
            vmem((2, 4, 64, 128), BF), vmem((2, 4, 64, 128), BF),
            vmem((8, 128), i32), smem((8, 128), i32), vmem((8, 128), i32), smem((8, 128), i32),
            vmem((2, 8, 128), i32), smem((8, 128), i32),
            vmem((17, 128, 512), BF), vmem((1024, 512), BF), vmem((32, 128, 128), BF),
            vmem((128, 512), BF), vmem((512, 512), BF), vmem((8, 64, 1024), BF),
            vmem((8, 1, 1024), F32), vmem((5, 192, 1280), BF), vmem((4, 192, 1280), BF),
            vmem((8, 64, 1024), BF), vmem((512, 512), BF), vmem((64, 64, 128), BF),
            vmem((3, 192, 192), BF), vmem((3, 192, 192), BF), vmem((128, 512), BF), vmem((512, 128), BF),
            vmem((128, 512), BF), vmem((128, 512), BF), vmem((17, 128, 128), BF),
            vmem((8, 64, 1024), BF), vmem((3, 192, 192), F32),
            vmem((8, 128, 512), BF), vmem((8, 64, 512), BF), vmem((27, 64, 64), F32),
            vmem((1536, 128), F32), vmem((3, 256, 128), F32), vmem((3, 256, 128), F32),
            vmem((3, 3, 64, 128), F32), vmem((3, 4, 64, 128), F32), vmem((3, 4, 64, 128), F32),
            vmem((1536, 128), BF), vmem((512, 128), F32),
            dma((2, 8)), dma((2, 8)), dma((3,)), dma((3,)), dma((18,)), dma((4,)), dma((4,)),
            dma((42,)), dma((42,)),
        ],
        compiler_params=pltpu.CompilerParams(
            collective_id=0, has_side_effects=True, vmem_limit_bytes=60 * 1024 * 1024
        ),
        cost_estimate=pl.CostEstimate(flops=6 * 10**9, bytes_accessed=12 * 10**6, transcendentals=10**6),
        name="sparse_conv",
    )(
        neighbors, occupancy, features, coarse_dest.reshape(1, 8), w_sub,
        w_down.transpose(0, 2, 1), coarse_grad, *constants,
    )
    return coarse, feat_grad, ws, wd.reshape(8, 64, 128).transpose(0, 2, 1)


def solution(mesh):
    return jax.shard_map(
        shards,
        mesh=mesh,
        in_specs=(
            P(("gz", "gy"), None, None),
            P(("gz", "gy"), None),
            P(("gz", "gy"), None),
            P(("gz", "gy")),
            P(),
            P(),
            P(("gz", "gy"), None, None),
        ),
        out_specs=(P(("gz", "gy"), None, None), P(("gz", "gy"), None, None), P(), P()),
        check_vma=False,
    )
```

```python
import functools

import jax
import jax.numpy as jnp
import numpy as np
from jax import lax
from jax.experimental import pallas as pl
from jax.experimental.pallas import tpu as pltpu
from jax.sharding import PartitionSpec as P

MESH = pl.DeviceIdType.MESH
BF = jnp.bfloat16
F32 = jnp.float32

Y_LOW, Y_HIGH, ZERO, Z_LOW, Z_HIGH, DIAGONAL, BANK = 64, 128, 192, 200, 208, 216, 248


def one_hot(shape, pairs):
    out = np.zeros(shape, np.float32)
    for row, column in pairs:
        out[row, column] = 1.0
    return jnp.asarray(out, BF)


def lane(y, x):
    return 10 * (y + 1) + x + 1


def permutations():
    wrap = [
        (64 * h + 8 * ((yp - 1) % 8) + (xp - 1) % 8, 128 * h + 10 * yp + xp)
        for h in range(2) for yp in range(10) for xp in range(10)
    ]
    rewrap = [
        (lane((yp - 1) % 8, (xp - 1) % 8), 10 * yp + xp) for yp in range(10) for xp in range(10)
    ]
    native = [
        (128 * h + lane(y, x), 64 * h + 8 * y + x)
        for h in range(2) for y in range(8) for x in range(8)
    ]
    pack = [
        (128 * z + 90 * side + x + 1, 64 * side + 8 * z + x)
        for side in range(2) for z in range(8) for x in range(8)
    ]
    unpack = [
        [
            (64 * parity + 8 * z + (xp - 1) % 8, 1024 * parity + 128 * z + 90 * side + xp)
            for parity in range(2) for z in range(8) for xp in range(10)
        ]
        for side in range(2)
    ]
    phase, octant = [], []
    for z in range(8):
        for y in range(8):
            for x in range(8):
                k = 4 * (z % 2) + 2 * (y % 2) + x % 2
                v = 16 * (z // 2) + 4 * (y // 2) + x // 2
                phase.append((128 * z + lane(y, x), 64 * k + v))
                k = 4 * (z // 4) + 2 * (y // 4) + x // 4
                v = 16 * (z % 4) + 4 * (y % 4) + x % 4
                octant.append((64 * k + v, 64 * z + 8 * y + x))
    flip = lambda pairs: [(b, a) for a, b in pairs]
    return (
        one_hot((128, 256), wrap),
        one_hot((128, 128), rewrap),
        one_hot((256, 128), native),
        one_hot((1024, 128), pack),
        one_hot((128, 2048), unpack[0]),
        one_hot((128, 2048), unpack[1]),
        one_hot((1024, 512), phase),
        one_hot((512, 1024), flip(phase)),
        one_hot((512, 512), octant),
        one_hot((512, 512), flip(octant)),
    )


def dot(a, b):
    return jnp.dot(a, b, preferred_element_type=F32)


def dot_nt(a, b):
    return lax.dot_general(a, b, (((1,), (1,)), ((), ())), preferred_element_type=F32)


def roll(x, shift):
    return pltpu.roll(x, shift % 128, x.ndim - 1)


PERMUTATIONS = ("wrap", "rewrap", "native", "pack", "un0", "un1", "phase", "unphase", "oct", "unoct")


def body(scale, *refs):
    operands, results, scratch = refs[:17], refs[17:21], refs[21:]
    nbr_h, occ_h, feat_h, dest_h, w_sub_h, w_down_h, cgrad = operands[:7]
    coarse, feat_grad, ws_out, wd_out = results
    nbr, occ, feat, dest_v, dest_s, w_sub, w_down = scratch[:7]
    p_wrap, p_rewrap, p_native, p_pack, p_un0, p_un1, p_phase, p_unphase, p_oct, p_unoct = scratch[7:17]
    (
        bank1, bank2, ysend, ydst, zsend, dsend, drecv, idx_v, idx_s, inv_v, inv_s, dest_buf, dest_in,
        cg_bank, og_in, og_all, og, ag_ph, ag, occ_p, r0, r1, act, phases, pg, wf, wb, wd, wdt,
        bl, bl_in, bl_bank, fg, wg, coarse_v, feat_v, ws_v,
        src, rc, s1, t1, t2, t3, fin, wd_v,
        h_send, h_recv, c_send, c_recv, in_sem, idx_sem, out_sem, r_send, r_recv,
    ) = scratch[17:]
    gz, gy = lax.axis_index("gz"), lax.axis_index("gy")
    cy, cz, core = gz // 8, (gz // 2) % 4, gz % 2
    nz, ny = 32, 4

    def at(dz, dy):
        return {"gz": (gz + dz + nz) % nz, "gy": (gy + dy + ny) % ny}

    def along(axis, d):
        if axis == 0:
            return {"gz": gz, "gy": (gy + d) % 4}
        if axis == 1:
            return {"gz": ((cy + d) % 4 * 4 + cz) * 2 + core, "gy": gy}
        return {"gz": (cy * 4 + (cz + d) % 4) * 2 + core, "gy": gy}

    coordinate = (gy, cy, cz)
    partner = {"gz": gz + 1 - 2 * core, "gy": gy}
    halo_steps = [(dz, dy) for dz in (-1, 0, 1) for dy in (-1, 0, 1) if (dz, dy) != (0, 0)]
    barrier = pltpu.get_barrier_semaphore()
    greeted = [at(*s) for s in halo_steps] + [partner]
    greeted += [along(axis, d) for axis in range(3) for d in (1, 2, 3)]
    for device in greeted:
        pl.semaphore_signal(barrier, inc=1, device_id=device, device_id_type=MESH)

    loads = {}

    def load(name, source, target):
        loads[name] = pltpu.make_async_copy(source, target, in_sem.at[len(loads)])
        loads[name].start()

    permuting = dict(zip(PERMUTATIONS, zip(operands[7:], scratch[7:17])))
    load("feat", feat_h, feat)
    load("occ", occ_h, occ)
    load("wrap", *permuting["wrap"])
    load("nbr", nbr_h, nbr)
    load("dest", dest_h, dest_v)
    load("dest_s", dest_h, dest_s)
    load("pack", *permuting["pack"])
    load("w_sub", w_sub_h, w_sub)
    load("w_down", w_down_h, w_down)
    load("cgrad", cgrad, cg_bank.at[pl.ds(0, 8)])
    for name in ("unoct", "unphase", "un0", "un1", "rewrap", "phase", "native", "oct"):
        load(name, *permuting[name])

    def send(src, dst, send_sem, recv_sem, device):
        copy = pltpu.make_async_remote_copy(
            src_ref=src, dst_ref=dst, send_sem=send_sem, recv_sem=recv_sem,
            device_id=device, device_id_type=MESH,
        )
        copy.start()
        return copy

    lanes = lax.broadcasted_iota(jnp.int32, (64, 128), 1)
    low_half = lax.broadcasted_iota(jnp.int32, (128, 128), 1) < 64
    xp = lanes - 10 * lax.shift_right_logical(lanes * 205, 11)
    first, last = xp == 0, xp == 9
    low64 = lanes < 64
    yp_low, yp_high = lanes < 10, lanes >= 90
    center_row = lax.broadcasted_iota(jnp.int32, (8, 128), 1)
    center_x = center_row - 10 * lax.shift_right_logical(center_row * 205, 11)
    center = (center_row > 10) & (center_row < 89) & (center_x > 0) & (center_x < 9)

    loads["nbr"].wait()
    table = nbr[...]
    owner = table // 8
    slot = table - owner * 8
    step_z = owner // 4 - gz
    step_y = owner - owner // 4 * 4 - gy
    column = lax.broadcasted_iota(jnp.int32, (8, 27), 1)
    part_a = column // 9
    edge_z = jnp.where(part_a == 0, 7, 0)
    on_z = Z_LOW + jnp.where(step_z > 0, 8, 0) + slot
    on_diagonal = DIAGONAL + jnp.where(step_z > 0, 16, 0) + jnp.where(step_y > 0, 8, 0) + slot
    same_z = jnp.where(step_y == 0, 0, jnp.where(step_y < 0, Y_LOW, Y_HIGH)) + slot * 8 + edge_z
    index = jnp.where(step_z == 0, same_z, jnp.where(step_y == 0, on_z, on_diagonal))
    index = jnp.where((table < 0) | ((part_a == 1) & (index > ZERO)), ZERO, index)
    idx_v[...] = jnp.zeros_like(idx_v)
    idx_v[:, 0:27] = index
    idx_copy = pltpu.make_async_copy(idx_v, idx_s, idx_sem.at[0])
    idx_copy.start()

    loads["feat"].wait()
    loads["occ"].wait()
    loads["wrap"].wait()
    for q in range(4):
        part = feat[:, :, 128 * q:128 * q + 128]
        flag = occ[:, 128 * q:128 * q + 128].astype(F32).astype(BF)
        rows = [part[t] * flag[t:t + 1] for t in range(8)]
        planes = dot(jnp.concatenate(rows, axis=0), p_wrap[...]).astype(BF)
        flags = dot(flag, p_wrap[...])
        for h in range(2):
            flag_plane = jnp.where(center, flags[:, 128 * h:128 * h + 128], 0.0)
            for t in range(8):
                occ_p[t, :, 128 * (2 * q + h):128 * (2 * q + h) + 128] = flag_plane[t:t + 1]
                bank1[8 * t + 2 * q + h] = planes[64 * t:64 * t + 64, 128 * h:128 * h + 128]

    loads["dest"].wait()
    dest_buf[0] = jnp.zeros((8, 128), jnp.int32) - 1
    dest_buf[0, 0:1, 0:8] = dest_v[...]
    for bank in (bank1, bank2):
        bank[ZERO:ZERO + 8] = jnp.zeros((8, 64, 128), BF)
    loads["pack"].wait()

    pl.semaphore_wait(barrier, len(greeted))
    dest_send = send(dest_buf.at[0], dest_buf.at[1], c_send.at[0], c_recv.at[0], partner)
    cg_send = send(cgrad, cg_bank.at[pl.ds(8, 8)], c_send.at[1], c_recv.at[1], partner)

    def publish(bank, which):
        copies = []
        total = None
        for q in range(4):
            both = jnp.concatenate(
                [
                    jnp.concatenate([bank[8 * t + 2 * q], bank[8 * t + 2 * q + 1]], axis=1)
                    for t in range(8)
                ],
                axis=0,
            )
            term = dot(both, p_pack[256 * q:256 * q + 256, :])
            total = term if total is None else total + term
        for j in range(4):
            even, odd = total[128 * j:128 * j + 64], total[128 * j + 64:128 * j + 128]
            ysend[which, 0, j] = jnp.where(low64, even, roll(odd, 64)).astype(BF)
            ysend[which, 1, j] = jnp.where(low64, roll(even, 64), odd).astype(BF)
        for side in range(2):
            for t in range(8):
                zsend[which, side, t] = bank[8 * t + (7 if side == 0 else 0)]
        for side in range(2):
            up = 1 - 2 * side
            copies.append(
                send(
                    ysend.at[which, side], ydst.at[which, side],
                    h_send.at[which, side], h_recv.at[which, side], at(0, up),
                )
            )
            copies.append(
                send(
                    zsend.at[which, side], bank.at[pl.ds(Z_LOW if side == 0 else Z_HIGH, 8)],
                    h_send.at[which, 2 + side], h_recv.at[which, 2 + side], at(up, 0),
                )
            )
        for side_z in range(2):
            for side_y in range(2):
                number = 2 * side_z + side_y
                gathered = None
                for t in range(8):
                    piece = bank[8 * t + (7 if side_z == 0 else 0)].astype(F32)
                    piece = roll(piece, 16 * t - 90 * side_y)
                    piece = jnp.where((lanes >= 16 * t) & (lanes < 16 * t + 10), piece, 0.0)
                    gathered = piece if gathered is None else gathered + piece
                dsend[which, number] = gathered.astype(BF)
                copies.append(
                    send(
                        dsend.at[which, number], drecv.at[which, number],
                        h_send.at[which, 4 + number], h_recv.at[which, 4 + number],
                        at(1 - 2 * side_z, 1 - 2 * side_y),
                    )
                )
        return copies

    def receive(bank, which, copies):
        for copy in copies:
            copy.wait_recv()
        for side in range(2):
            rows = ydst[which, side].reshape(256, 128)
            for q in range(8):
                planes = dot(rows, (p_un0, p_un1)[side][:, 256 * q:256 * q + 256]).astype(BF)
                for j in range(4):
                    for h in range(2):
                        t, z = 2 * j + q // 4, 2 * (q % 4) + h
                        bank[(Y_LOW, Y_HIGH)[side] + 8 * t + z] = planes[
                            64 * j:64 * j + 64, 128 * h:128 * h + 128
                        ]
        for side_z in range(2):
            for side_y in range(2):
                number = 2 * side_z + side_y
                packed = drecv[which, number].astype(F32)
                for t in range(8):
                    bank[DIAGONAL + 8 * number + t] = roll(packed, 90 * side_y - 16 * t).astype(BF)

    def assemble(bank, t, r_buf, i, planes):
        for zp in planes:
            a = 0 if zp == 0 else (2 if zp == 9 else 1)
            rows = []
            for b in range(3):
                loaded = []
                for c in range(3):
                    place = idx_s[t, 9 * a + 3 * b + c] + (zp - 1 if a == 1 else 0)
                    loaded.append(bank[place])
                rows.append(jnp.where(first, loaded[0], jnp.where(last, loaded[2], loaded[1])))
            plane = jnp.where(yp_low, rows[0], jnp.where(yp_high, rows[2], rows[1]))
            wide = plane.astype(F32)
            columns = slice(128 * zp, 128 * zp + 128)
            r_buf[i, 0:64, columns] = roll(wide, 10).astype(BF)
            r_buf[i, 64:128, columns] = plane
            r_buf[i, 128:192, columns] = roll(wide, -10).astype(BF)

    def convolve(weights, r_buf, i, q):
        total = None
        for a in range(3):
            term = dot(weights[a], r_buf[i, :, 128 * a + 256 * q:128 * a + 256 * q + 256])
            total = term if total is None else total + term
        parts = []
        for h in range(2):
            y = total[:, 128 * h:128 * h + 128]
            parts.append(roll(y[0:64], 1) + y[64:128] + roll(y[128:192], -1))
        return parts

    groups = ((0, 1, 2), (3, 4, 5), (6, 7), (8, 9))

    def sweep(bank, low, high, tile):
        if low == 0:
            for planes in groups:
                assemble(bank, 0, r0, 0, planes)

        @pl.loop(low, high)
        def _(i):
            for q in range(4):
                assemble(bank, 2 * i + 1, r1, i, groups[q])
                tile(r0, i, 2 * i, q)
            for q in range(4):
                assemble(bank, jnp.minimum(2 * i + 2, 7), r0, i + 1, groups[q])
                tile(r1, i, 2 * i + 1, q)

    halo = publish(bank1, 0)

    loads["w_sub"].wait()
    loads["w_down"].wait()
    for a in range(3):
        for c in range(3):
            wf[a, 64 * c:64 * c + 64, :] = jnp.concatenate(
                [w_sub[9 * a + 3 * b + c].astype(F32) for b in range(3)], axis=1
            ).astype(BF)
        turned = jnp.concatenate(
            [
                jnp.concatenate(
                    [w_sub[9 * (2 - a) + 3 * (2 - b) + 2 - c].astype(F32) for c in range(3)], axis=1
                )
                for b in range(3)
            ],
            axis=0,
        )
        wb[a] = turned.T.astype(BF)
    wdt[...] = w_down[...].reshape(512, 128)
    wd[...] = wdt[...].astype(F32).T.astype(BF)

    cg_bank[16] = jnp.zeros((128, 512), BF)
    idx_copy.wait()
    loads["dest_s"].wait()
    loads["cgrad"].wait()
    loads["unoct"].wait()
    cg_send.wait_recv()
    base = gz * 4 + gy
    partner_index = (gz + 1 - 2 * core) * 4 + gy
    for t in range(8):
        d = dest_s[0, t]
        own = d // 8 - base * 8
        other = d // 8 - partner_index * 8
        chosen = jnp.where((other >= 0) & (other < 8), 8 + other, 16)
        chosen = jnp.where((own >= 0) & (own < 8), own, chosen)
        og_in[128 * t:128 * t + 128, :] = cg_bank[chosen]
    for q in range(2):
        split = dot(og_in[...], p_unoct[:, 256 * q:256 * q + 256]).astype(BF)
        for t in range(8):
            for h in range(2):
                og_all[4 * t + 2 * q + h] = split[128 * t:128 * t + 128, 128 * h:128 * h + 128]
    for j in range(4):
        halves = []
        for h in range(2):
            t = 2 * j + h
            d = dest_s[0, t]
            octant = d - d // 8 * 8
            piece = og_all[4 * t + octant // 2].astype(F32)
            odd = octant - octant // 2 * 2
            halves.append(jnp.where(odd == h, piece, roll(piece, 64)))
        og[:, 128 * j:128 * j + 128] = jnp.where(low_half, halves[0], halves[1]).astype(BF)
    for r in range(4):
        rows = dot(wdt[128 * r:128 * r + 128, :], og[...]).astype(BF).astype(F32)
        for j in range(4):
            even = rows[0:64, 128 * j:128 * j + 128]
            odd = rows[64:128, 128 * j:128 * j + 128]
            columns = slice(128 * r, 128 * r + 128)
            ag_ph[128 * j:128 * j + 64, columns] = jnp.where(low64, even, roll(odd, 64)).astype(BF)
            ag_ph[128 * j + 64:128 * j + 128, columns] = jnp.where(
                low64, roll(even, 64), odd
            ).astype(BF)
    loads["unphase"].wait()
    for q in range(4):
        spread = dot(ag_ph[...], p_unphase[:, 256 * q:256 * q + 256]).astype(BF)
        for t in range(8):
            ag[t, :, 256 * q:256 * q + 256] = spread[64 * t:64 * t + 64]

    dest_send.wait_recv()
    dest_copy = pltpu.make_async_copy(dest_buf.at[1], dest_in, idx_sem.at[2])
    dest_copy.start()
    dest_copy.wait()
    place = lax.broadcasted_iota(jnp.int32, (8, 128), 1) + base * 64
    inverse = jnp.zeros((8, 128), jnp.int32) + 16
    for s in range(8):
        inverse = jnp.where(place == dest_s[0, s], s, inverse)
        inverse = jnp.where(place == dest_in[0, s], 8 + s, inverse)
    inv_v[...] = inverse
    inv_copy = pltpu.make_async_copy(inv_v, inv_s, idx_sem.at[3])
    inv_copy.start()

    loads["un0"].wait()
    loads["un1"].wait()
    receive(bank1, 0, halo)

    def forward(r_buf, i, t, q):
        parts = convolve(wf, r_buf, i, q)
        for h in range(2):
            z = 2 * q + h
            v = parts[h]
            on = occ_p[t, :, 128 * z:128 * z + 128]
            s = 1.0 / (1.0 + jnp.exp(-v))
            act[t, :, 128 * z:128 * z + 128] = jnp.where(on > 0.5, v * s, 0.0).astype(BF)
            g = ag[t, :, 128 * z:128 * z + 128].astype(F32)
            g = g * s * (1.0 + v * (1.0 - s))
            pg[8 * t + z] = jnp.where(on > 0.5, g, 0.0).astype(BF)

    sweep(bank1, 0, 4, forward)

    wg[...] = jnp.zeros_like(wg)

    @pl.loop(0, 4)
    def _(i):
        for h in range(2):
            planes = [pg[8 * (2 * i + h) + z].astype(F32) for z in range(8)]
            shifted = jnp.concatenate(
                [
                    jnp.concatenate([roll(p, c - 1).astype(BF) for p in planes], axis=1)
                    for c in range(3)
                ],
                axis=0,
            )
            for a in range(3):
                wg[a] += dot_nt(shifted, (r0, r1)[h][i, :, 128 * a:128 * a + 1024])

    for a in range(3):
        src[192 * a:192 * a + 192, :] = wg[a, :, 0:128]
    src[576:768, :] = jnp.concatenate([wg[0, :, 128:192], wg[1, :, 128:192]], axis=1)
    src[768:960, 0:64] = wg[2, :, 128:192]
    src[768:960, 64:128] = jnp.zeros((192, 64), F32)
    src[960:1024, :] = jnp.zeros((64, 128), F32)


    def pair(n):
        return r_send.at[n], r_recv.at[n]

    def rows_at(start, size):
        return pl.ds(pl.multiple_of(start, 8), size)

    def axis_of(p, stage):
        return (p + stage) % 3

    def me(p, stage):
        return coordinate[axis_of(p, stage)]

    def first_row(p, half):
        return 512 * half + 256 * p if p < 2 else 1024 + 256 * half

    def stage_0(p, _):
        rows = rows_at(first_row(p, 1 - core), 256)
        return [send(src.at[rows], rc.at[p], *pair(p), partner)]

    def arrived(copies):
        for copy in copies:
            copy.wait_recv()

    def stage_1(p, before):
        arrived(before)
        s1[p] = src[rows_at(first_row(p, core), 256)] + rc[p]
        copies = []
        for d in (1, 2, 3):
            to = (me(p, 0) + d) % 4
            copies.append(
                send(
                    s1.at[p, rows_at(64 * to, 64)], t1.at[p, d - 1],
                    *pair(3 + 3 * p + d - 1), along(axis_of(p, 0), d),
                )
            )
        return copies

    def exchange(buffer, p, stage, value, first_pair):
        buffer[p, me(p, stage)] = value
        place = buffer.at[p, me(p, stage)]
        return [
            send(place, place, *pair(first_pair + 3 * p + d - 1), along(axis_of(p, stage), d))
            for d in (1, 2, 3)
        ]

    def stage_2(p, before):
        arrived(before)
        total = s1[p, rows_at(64 * me(p, 0), 64)]
        for d in range(3):
            total = total + t1[p, d]
        return exchange(t2, p, 1, total, 12)

    def stage_3(p, before):
        arrived(before)
        return exchange(t3, p, 2, (t2[p, 0] + t2[p, 1]) + (t2[p, 2] + t2[p, 3]), 21)

    def stage_4(p, before):
        arrived(before)
        rows = rows_at(first_row(p, core) + 64 * me(p, 0), 64)
        total = (t3[p, 0] + t3[p, 1]) + (t3[p, 2] + t3[p, 3])
        fin[rows] = (total * scale).astype(BF)
        return [
            send(fin.at[rows], fin.at[rows], *pair(30 + 3 * p + d - 1), along(axis_of(p, 0), d))
            for d in (1, 2, 3)
        ]

    def stage_5(p, before):
        arrived(before)
        rows = rows_at(first_row(p, core), 256)
        return [send(fin.at[rows], fin.at[rows], *pair(39 + p), partner)]

    stages = [stage_0, stage_1, stage_2, stage_3, stage_4, stage_5]
    reduced = [[], [], []]

    def reduce_step(*parts):
        for p in parts:
            n = len(reduced[p])
            reduced[p].append(stages[n](p, reduced[p][-1] if n > 0 else None))

    loads["phase"].wait()
    for q in range(2):
        split = dot(act[...].reshape(512, 1024), p_phase[:, 256 * q:256 * q + 256])
        for j in range(4):
            for h in range(2):
                even = split[128 * j:128 * j + 64, 128 * h:128 * h + 128]
                odd = split[128 * j + 64:128 * j + 128, 128 * h:128 * h + 128]
                k = 4 * q + 2 * h
                columns = slice(128 * j, 128 * j + 128)
                phases[64 * k:64 * k + 64, columns] = jnp.where(
                    low64, even, roll(odd, 64)
                ).astype(BF)
                phases[64 * k + 64:64 * k + 128, columns] = jnp.where(
                    low64, roll(even, 64), odd
                ).astype(BF)
    src[1024:1536, :] = dot_nt(phases[...], og[...])

    reduce_step(0, 1, 2)
    bl[...] = dot(wd[...], phases[...]).astype(BF)
    bl_send = send(bl, bl_in, c_send.at[2], c_recv.at[2], partner)

    loads["rewrap"].wait()
    for t in range(8):
        rows = pg[8 * t:8 * t + 8].reshape(512, 128)
        bank2[8 * t:8 * t + 8] = dot(rows, p_rewrap[...]).astype(BF).reshape(8, 64, 128)

    reduce_step(0, 1, 2)
    halo2 = publish(bank2, 1)

    inv_copy.wait()
    bl_send.wait_recv()
    bl_bank[16] = jnp.zeros((128, 128), BF)
    for source in range(2):
        blocks = (bl, bl_in)[source]
        for j in range(4):
            both = blocks[:, 128 * j:128 * j + 128].astype(F32)
            turned = roll(both, 64)
            bl_bank[8 * source + 2 * j] = jnp.where(low_half, both, turned).astype(BF)
            bl_bank[8 * source + 2 * j + 1] = jnp.where(low_half, turned, both).astype(BF)
    for c in range(8):
        for q in range(4):
            even = bl_bank[inv_s[0, 8 * c + 2 * q]]
            odd = bl_bank[inv_s[0, 8 * c + 2 * q + 1]]
            og_in[128 * c:128 * c + 128, 128 * q:128 * q + 128] = jnp.where(low_half, even, odd)
    loads["oct"].wait()
    for q in range(2):
        rows = dot(og_in[...], p_oct[:, 256 * q:256 * q + 256]).astype(BF)
        coarse_v[:, :, 256 * q:256 * q + 256] = rows.reshape(8, 128, 256)
    coarse_out = pltpu.make_async_copy(coarse_v, coarse, out_sem.at[1])
    coarse_out.start()
    reduce_step(0, 1, 2)
    receive(bank2, 1, halo2)
    reduce_step(0, 1, 2)

    def backward(r_buf, i, t, q):
        parts = convolve(wb, r_buf, i, q)
        for h in range(2):
            z = 2 * q + h
            on = occ_p[t, :, 128 * z:128 * z + 128]
            fg[t, :, 128 * z:128 * z + 128] = jnp.where(on > 0.5, parts[h], 0.0).astype(BF)

    sweep(bank2, 0, 2, backward)
    reduce_step(0, 1, 2)
    sweep(bank2, 2, 4, backward)
    reduce_step(0, 1, 2)
    loads["native"].wait()
    for q in range(4):
        rows = dot(fg[:, :, 256 * q:256 * q + 256].reshape(512, 256), p_native[...])
        feat_v[:, :, 128 * q:128 * q + 128] = rows.astype(BF).reshape(8, 64, 128)
    feat_out = pltpu.make_async_copy(feat_v, feat_grad, out_sem.at[0])
    feat_out.start()

    arrived(reduced[0][5] + reduced[1][5])
    for a in range(3):
        for c in range(3):
            for b in range(2):
                rows = slice(192 * a + 64 * c, 192 * a + 64 * c + 64)
                ws_v[9 * a + 3 * b + c] = fin[rows, 64 * b:64 * b + 64].astype(F32)
            row, column = ((576, 0), (576, 64), (768, 0))[a]
            rows = slice(row + 64 * c, row + 64 * c + 64)
            ws_v[9 * a + 6 + c] = fin[rows, column:column + 64].astype(F32)
    sub_out = pltpu.make_async_copy(ws_v, ws_out, out_sem.at[3])
    sub_out.start()
    arrived(reduced[2][5])
    wd_v[...] = fin[1024:1536, :].astype(F32)
    down_out = pltpu.make_async_copy(wd_v, wd_out, out_sem.at[2])
    down_out.start()
    for copy in halo + halo2 + [dest_send, cg_send, bl_send]:
        copy.wait_send()
    for stage in reduced:
        for copies in stage:
            for copy in copies:
                copy.wait_send()
    for copy in (feat_out, coarse_out, down_out, sub_out):
        copy.wait()


def write_out(*refs):
    sources, targets, sems = refs[:4], refs[4:8], refs[8]
    copies = [pltpu.make_async_copy(a, b, sems.at[n]) for n, (a, b) in enumerate(zip(sources, targets))]
    for copy in copies:
        copy.start()
    for copy in copies:
        copy.wait()


def shards(features, occupancy, neighbors, coarse_dest, w_sub, w_down, coarse_grad):
    devices = lax.axis_size("gz") * lax.axis_size("gy")
    scale = (features.shape[0] * devices * 512.0) ** -0.5
    anywhere = pl.BlockSpec(memory_space=pl.ANY)
    constants = permutations()
    vmem, smem, dma = pltpu.VMEM, pltpu.SMEM, pltpu.SemaphoreType.DMA
    i32 = jnp.int32
    held = pl.pallas_call(
        functools.partial(body, scale),
        out_shape=(
            vmem((8, 128, 512), BF), vmem((8, 64, 512), BF), vmem((27, 64, 64), F32), vmem((512, 128), F32),
        ),
        in_specs=[anywhere] * 17,
        out_specs=(anywhere,) * 4,
        scratch_shapes=[
            vmem((8, 27), i32), vmem((8, 512), i32), vmem((8, 64, 512), BF), vmem((1, 8), i32),
            smem((1, 8), i32), vmem((27, 64, 64), BF), vmem((8, 64, 128), BF),
        ] + [vmem(c.shape, BF) for c in constants] + [
            vmem((BANK, 64, 128), BF), vmem((BANK, 64, 128), BF),
            vmem((2, 2, 4, 64, 128), BF), vmem((2, 2, 4, 64, 128), BF), vmem((2, 2, 8, 64, 128), BF),
            vmem((2, 4, 64, 128), BF), vmem((2, 4, 64, 128), BF),
            vmem((8, 128), i32), smem((8, 128), i32), vmem((8, 128), i32), smem((8, 128), i32),
            vmem((2, 8, 128), i32), smem((8, 128), i32),
            vmem((17, 128, 512), BF), vmem((1024, 512), BF), vmem((32, 128, 128), BF),
            vmem((128, 512), BF), vmem((512, 512), BF), vmem((8, 64, 1024), BF),
            vmem((8, 1, 1024), F32), vmem((5, 192, 1280), BF), vmem((4, 192, 1280), BF),
            vmem((8, 64, 1024), BF), vmem((512, 512), BF), vmem((64, 64, 128), BF),
            vmem((3, 192, 192), BF), vmem((3, 192, 192), BF), vmem((128, 512), BF), vmem((512, 128), BF),
            vmem((128, 512), BF), vmem((128, 512), BF), vmem((17, 128, 128), BF),
            vmem((8, 64, 1024), BF), vmem((3, 192, 192), F32),
            vmem((8, 128, 512), BF), vmem((8, 64, 512), BF), vmem((27, 64, 64), F32),
            vmem((1536, 128), F32), vmem((3, 256, 128), F32), vmem((3, 256, 128), F32),
            vmem((3, 3, 64, 128), F32), vmem((3, 4, 64, 128), F32), vmem((3, 4, 64, 128), F32),
            vmem((1536, 128), BF), vmem((512, 128), F32),
            dma((2, 8)), dma((2, 8)), dma((3,)), dma((3,)), dma((18,)), dma((4,)), dma((4,)),
            dma((42,)), dma((42,)),
        ],
        compiler_params=pltpu.CompilerParams(
            collective_id=0, has_side_effects=True, vmem_limit_bytes=60 * 1024 * 1024
        ),
        cost_estimate=pl.CostEstimate(flops=6 * 10**9, bytes_accessed=12 * 10**6, transcendentals=10**6),
        name="sparse_conv",
    )(
        neighbors, occupancy, features, coarse_dest.reshape(1, 8), w_sub,
        w_down.transpose(0, 2, 1), coarse_grad, *constants,
    )
    coarse, feat_grad, ws, wd = pl.pallas_call(
        write_out,
        out_shape=[jax.ShapeDtypeStruct(x.shape, x.dtype) for x in held],
        in_specs=[anywhere] * 4,
        out_specs=[anywhere] * 4,
        scratch_shapes=[dma((4,))],
        compiler_params=pltpu.CompilerParams(vmem_limit_bytes=1024 * 1024),
        name="write_out",
    )(*held)
    return coarse, feat_grad, ws, wd.reshape(8, 64, 128).transpose(0, 2, 1)


def solution(mesh):
    return jax.shard_map(
        shards,
        mesh=mesh,
        in_specs=(
            P(("gz", "gy"), None, None),
            P(("gz", "gy"), None),
            P(("gz", "gy"), None),
            P(("gz", "gy")),
            P(),
            P(),
            P(("gz", "gy"), None, None),
        ),
        out_specs=(P(("gz", "gy"), None, None), P(("gz", "gy"), None, None), P(), P()),
        check_vma=False,
    )
```

```python
import functools

import jax
import jax.numpy as jnp
import numpy as np
from jax import lax
from jax.experimental import pallas as pl
from jax.experimental.pallas import tpu as pltpu
from jax.sharding import PartitionSpec as P

MESH = pl.DeviceIdType.MESH
BF = jnp.bfloat16
F32 = jnp.float32

Y_SIDES, ZERO, Z_LOW, Z_HIGH, DIAGONAL, BANK = 64, 128, 136, 144, 152, 168


def one_hot(shape, pairs):
    out = np.zeros(shape, np.float32)
    for row, column in pairs:
        out[row, column] = 1.0
    return jnp.asarray(out, BF)


def lane(y, x):
    return 10 * (y + 1) + x + 1


def permutations():
    wrap = [
        (64 * h + 8 * ((yp - 1) % 8) + (xp - 1) % 8, 128 * h + 10 * yp + xp)
        for h in range(2) for yp in range(10) for xp in range(10)
    ]
    rewrap = [
        (lane((yp - 1) % 8, (xp - 1) % 8), 10 * yp + xp) for yp in range(10) for xp in range(10)
    ]
    native = [
        (128 * h + lane(y, x), 64 * h + 8 * y + x)
        for h in range(2) for y in range(8) for x in range(8)
    ]
    pack = [
        (128 * z + 90 * side + x + 1, 64 * side + 8 * z + x)
        for side in range(2) for z in range(8) for x in range(8)
    ]
    unpack = [
        (128 * side + 64 * parity + 8 * z + (xp - 1) % 8, 1024 * parity + 128 * z + 90 * side + xp)
        for side in range(2) for parity in range(2) for z in range(8) for xp in range(10)
    ]
    phase, octant = [], []
    for z in range(8):
        for y in range(8):
            for x in range(8):
                k = 4 * (z % 2) + 2 * (y % 2) + x % 2
                v = 16 * (z // 2) + 4 * (y // 2) + x // 2
                phase.append((128 * z + lane(y, x), 64 * k + v))
                k = 4 * (z // 4) + 2 * (y // 4) + x // 4
                v = 16 * (z % 4) + 4 * (y % 4) + x % 4
                octant.append((64 * k + v, 64 * z + 8 * y + x))
    flip = lambda pairs: [(b, a) for a, b in pairs]
    return (
        one_hot((128, 256), wrap),
        one_hot((128, 128), rewrap),
        one_hot((256, 128), native),
        one_hot((1024, 128), pack),
        one_hot((256, 2048), unpack),
        one_hot((1024, 512), phase),
        one_hot((512, 1024), flip(phase)),
        one_hot((512, 512), octant),
        one_hot((512, 512), flip(octant)),
    )


def dot(a, b):
    return jnp.dot(a, b, preferred_element_type=F32)


def dot_nt(a, b):
    return lax.dot_general(a, b, (((1,), (1,)), ((), ())), preferred_element_type=F32)


def roll(x, shift):
    return pltpu.roll(x, shift % 128, x.ndim - 1)


PERMUTATIONS = ("wrap", "rewrap", "native", "pack", "unpack", "phase", "unphase", "oct", "unoct")


def body(scale, *refs):
    operands, results, scratch = refs[:16], refs[16:20], refs[20:]
    nbr_h, occ_h, feat_h, dest_h, w_sub_h, w_down_h, cgrad = operands[:7]
    coarse, feat_grad, ws_out, wd_out = results
    nbr, occ, feat, dest_v, dest_s, w_sub, w_down = scratch[:7]
    p_wrap, p_rewrap, p_native, p_pack, p_unpack, p_phase, p_unphase, p_oct, p_unoct = scratch[7:16]
    (
        bank1, bank2, ysend, ydst, zsend, dsend, drecv, idx_v, idx_s, inv_v, inv_s, dest_buf, dest_in,
        cg_bank, og_in, og_all, og, ag_ph, ag, occ_p, r0, r1, act, phases, pg, wf, wb, wd, wdt,
        bl, bl_in, bl_bank, fg, wg, coarse_v, feat_v, ws_v,
        src, rc, s1, t1, t2, t3, fin, wd_v,
        h_send, h_recv, c_send, c_recv, in_sem, idx_sem, out_sem, r_send, r_recv,
    ) = scratch[16:]
    gz, gy = lax.axis_index("gz"), lax.axis_index("gy")
    cy, cz, core = gz // 8, (gz // 2) % 4, gz % 2
    nz, ny = 32, 4

    def at(dz, dy):
        return {"gz": (gz + dz + nz) % nz, "gy": (gy + dy + ny) % ny}

    def along(axis, d):
        if axis == 0:
            return {"gz": gz, "gy": (gy + d) % 4}
        if axis == 1:
            return {"gz": ((cy + d) % 4 * 4 + cz) * 2 + core, "gy": gy}
        return {"gz": (cy * 4 + (cz + d) % 4) * 2 + core, "gy": gy}

    coordinate = (gy, cy, cz)
    partner = {"gz": gz + 1 - 2 * core, "gy": gy}
    halo_steps = [(dz, dy) for dz in (-1, 0, 1) for dy in (-1, 0, 1) if (dz, dy) != (0, 0)]
    barrier = pltpu.get_barrier_semaphore()
    greeted = [at(*s) for s in halo_steps] + [partner]
    greeted += [along(axis, d) for axis in range(3) for d in (1, 2, 3)]
    for device in greeted:
        pl.semaphore_signal(barrier, inc=1, device_id=device, device_id_type=MESH)

    loads = {}

    def load(name, source, target):
        loads[name] = pltpu.make_async_copy(source, target, in_sem.at[len(loads)])
        loads[name].start()

    permuting = dict(zip(PERMUTATIONS, zip(operands[7:], scratch[7:16])))
    load("feat", feat_h, feat)
    load("occ", occ_h, occ)
    load("wrap", *permuting["wrap"])
    load("nbr", nbr_h, nbr)
    load("dest", dest_h, dest_v)
    load("dest_s", dest_h, dest_s)
    load("pack", *permuting["pack"])
    load("w_sub", w_sub_h, w_sub)
    load("w_down", w_down_h, w_down)
    load("cgrad", cgrad, cg_bank.at[pl.ds(0, 8)])
    for name in ("unoct", "unphase", "unpack", "rewrap", "phase", "native", "oct"):
        load(name, *permuting[name])

    def send(src, dst, send_sem, recv_sem, device):
        copy = pltpu.make_async_remote_copy(
            src_ref=src, dst_ref=dst, send_sem=send_sem, recv_sem=recv_sem,
            device_id=device, device_id_type=MESH,
        )
        copy.start()
        return copy

    lanes = lax.broadcasted_iota(jnp.int32, (64, 128), 1)
    low_half = lax.broadcasted_iota(jnp.int32, (128, 128), 1) < 64
    xp = lanes - 10 * lax.shift_right_logical(lanes * 205, 11)
    first, last = xp == 0, xp == 9
    low64 = lanes < 64
    yp_low, yp_high = lanes < 10, lanes >= 90
    center_row = lax.broadcasted_iota(jnp.int32, (8, 128), 1)
    center_x = center_row - 10 * lax.shift_right_logical(center_row * 205, 11)
    center = (center_row > 10) & (center_row < 89) & (center_x > 0) & (center_x < 9)

    loads["nbr"].wait()
    table = nbr[...]
    owner = table // 8
    slot = table - owner * 8
    step_z = owner // 4 - gz
    step_y = owner - owner // 4 * 4 - gy
    column = lax.broadcasted_iota(jnp.int32, (8, 27), 1)
    part_a = column // 9
    edge_z = jnp.where(part_a == 0, 7, 0)
    on_z = Z_LOW + jnp.where(step_z > 0, 8, 0) + slot
    on_diagonal = DIAGONAL + jnp.where(step_z > 0, 8, 0) + slot
    same_z = jnp.where(step_y == 0, 0, Y_SIDES) + slot * 8 + edge_z
    index = jnp.where(step_z == 0, same_z, jnp.where(step_y == 0, on_z, on_diagonal))
    index = jnp.where((table < 0) | ((part_a == 1) & (index > ZERO)), ZERO, index)
    idx_v[...] = jnp.zeros_like(idx_v)
    idx_v[:, 0:27] = index
    idx_copy = pltpu.make_async_copy(idx_v, idx_s, idx_sem.at[0])
    idx_copy.start()

    loads["feat"].wait()
    loads["occ"].wait()
    loads["wrap"].wait()
    for q in range(4):
        part = feat[:, :, 128 * q:128 * q + 128]
        flag = occ[:, 128 * q:128 * q + 128].astype(F32).astype(BF)
        rows = [part[t] * flag[t:t + 1] for t in range(8)]
        planes = dot(jnp.concatenate(rows, axis=0), p_wrap[...]).astype(BF)
        flags = dot(flag, p_wrap[...])
        for h in range(2):
            flag_plane = jnp.where(center, flags[:, 128 * h:128 * h + 128], 0.0)
            for t in range(8):
                occ_p[t, :, 128 * (2 * q + h):128 * (2 * q + h) + 128] = flag_plane[t:t + 1]
                bank1[8 * t + 2 * q + h] = planes[64 * t:64 * t + 64, 128 * h:128 * h + 128]

    loads["dest"].wait()
    dest_buf[0] = jnp.zeros((8, 128), jnp.int32) - 1
    dest_buf[0, 0:1, 0:8] = dest_v[...]
    for bank in (bank1, bank2):
        bank[ZERO:ZERO + 8] = jnp.zeros((8, 64, 128), BF)
    loads["pack"].wait()

    pl.semaphore_wait(barrier, len(greeted))
    dest_send = send(dest_buf.at[0], dest_buf.at[1], c_send.at[0], c_recv.at[0], partner)
    cg_send = send(cgrad, cg_bank.at[pl.ds(8, 8)], c_send.at[1], c_recv.at[1], partner)

    def publish(bank, which):
        copies = []
        total = None
        for q in range(4):
            both = jnp.concatenate(
                [
                    jnp.concatenate([bank[8 * t + 2 * q], bank[8 * t + 2 * q + 1]], axis=1)
                    for t in range(8)
                ],
                axis=0,
            )
            term = dot(both, p_pack[256 * q:256 * q + 256, :])
            total = term if total is None else total + term
        for j in range(4):
            even, odd = total[128 * j:128 * j + 64], total[128 * j + 64:128 * j + 128]
            ysend[which, 0, j] = jnp.where(low64, even, roll(odd, 64)).astype(BF)
            ysend[which, 1, j] = jnp.where(low64, roll(even, 64), odd).astype(BF)
        for side in range(2):
            for t in range(8):
                zsend[which, side, t] = bank[8 * t + (7 if side == 0 else 0)]
        for side in range(2):
            up = 1 - 2 * side
            copies.append(
                send(
                    ysend.at[which, side], ydst.at[which, side],
                    h_send.at[which, side], h_recv.at[which, side], at(0, up),
                )
            )
            copies.append(
                send(
                    zsend.at[which, side], bank.at[pl.ds(Z_LOW if side == 0 else Z_HIGH, 8)],
                    h_send.at[which, 2 + side], h_recv.at[which, 2 + side], at(up, 0),
                )
            )
        for side_z in range(2):
            for side_y in range(2):
                number = 2 * side_z + side_y
                gathered = None
                for t in range(8):
                    piece = bank[8 * t + (7 if side_z == 0 else 0)].astype(F32)
                    piece = roll(piece, 16 * t - 90 * side_y)
                    piece = jnp.where((lanes >= 16 * t) & (lanes < 16 * t + 10), piece, 0.0)
                    gathered = piece if gathered is None else gathered + piece
                dsend[which, number] = gathered.astype(BF)
                copies.append(
                    send(
                        dsend.at[which, number], drecv.at[which, number],
                        h_send.at[which, 4 + number], h_recv.at[which, 4 + number],
                        at(1 - 2 * side_z, 1 - 2 * side_y),
                    )
                )
        return copies

    def receive(bank, which, copies):
        for copy in copies:
            copy.wait_recv()
        rows = jnp.concatenate([ydst[which, side].reshape(256, 128) for side in range(2)], axis=1)
        for q in range(8):
            planes = dot(rows, p_unpack[:, 256 * q:256 * q + 256]).astype(BF)
            for j in range(4):
                for h in range(2):
                    t, z = 2 * j + q // 4, 2 * (q % 4) + h
                    bank[Y_SIDES + 8 * t + z] = planes[64 * j:64 * j + 64, 128 * h:128 * h + 128]
        for side_z in range(2):
            below = drecv[which, 2 * side_z].astype(F32)
            above = drecv[which, 2 * side_z + 1].astype(F32)
            for t in range(8):
                bank[DIAGONAL + 8 * side_z + t] = jnp.where(
                    yp_low, roll(below, -16 * t), roll(above, 90 - 16 * t)
                ).astype(BF)

    def assemble(bank, t, r_buf, i, planes):
        for zp in planes:
            a = 0 if zp == 0 else (2 if zp == 9 else 1)
            rows = []
            for b in range(3):
                loaded = []
                for c in range(3):
                    place = idx_s[t, 9 * a + 3 * b + c] + (zp - 1 if a == 1 else 0)
                    loaded.append(bank[place])
                rows.append(jnp.where(first, loaded[0], jnp.where(last, loaded[2], loaded[1])))
            plane = jnp.where(yp_low, rows[0], jnp.where(yp_high, rows[2], rows[1]))
            wide = plane.astype(F32)
            columns = slice(128 * zp, 128 * zp + 128)
            r_buf[i, 0:64, columns] = roll(wide, 10).astype(BF)
            r_buf[i, 64:128, columns] = plane
            r_buf[i, 128:192, columns] = roll(wide, -10).astype(BF)

    def convolve(weights, r_buf, i, q):
        total = None
        for a in range(3):
            term = dot(weights[a], r_buf[i, :, 128 * a + 256 * q:128 * a + 256 * q + 256])
            total = term if total is None else total + term
        parts = []
        for h in range(2):
            y = total[:, 128 * h:128 * h + 128]
            parts.append(roll(y[0:64], 1) + y[64:128] + roll(y[128:192], -1))
        return parts

    groups = ((0, 1, 2), (3, 4, 5), (6, 7), (8, 9))

    def sweep(bank, low, high, tile):
        if low == 0:
            for planes in groups:
                assemble(bank, 0, r0, 0, planes)

        @pl.loop(low, high)
        def _(i):
            for q in range(4):
                assemble(bank, 2 * i + 1, r1, i, groups[q])
                tile(r0, i, 2 * i, q)
            for q in range(4):
                assemble(bank, jnp.minimum(2 * i + 2, 7), r0, i + 1, groups[q])
                tile(r1, i, 2 * i + 1, q)

    halo = publish(bank1, 0)

    loads["w_sub"].wait()
    loads["w_down"].wait()
    for a in range(3):
        for c in range(3):
            wf[a, 64 * c:64 * c + 64, :] = jnp.concatenate(
                [w_sub[9 * a + 3 * b + c].astype(F32) for b in range(3)], axis=1
            ).astype(BF)
        turned = jnp.concatenate(
            [
                jnp.concatenate(
                    [w_sub[9 * (2 - a) + 3 * (2 - b) + 2 - c].astype(F32) for c in range(3)], axis=1
                )
                for b in range(3)
            ],
            axis=0,
        )
        wb[a] = turned.T.astype(BF)
    wdt[...] = w_down[...].reshape(512, 128)
    wd[...] = wdt[...].astype(F32).T.astype(BF)

    cg_bank[16] = jnp.zeros((128, 512), BF)
    idx_copy.wait()
    loads["dest_s"].wait()
    loads["cgrad"].wait()
    loads["unoct"].wait()
    cg_send.wait_recv()
    base = gz * 4 + gy
    partner_index = (gz + 1 - 2 * core) * 4 + gy
    for t in range(8):
        d = dest_s[0, t]
        own = d // 8 - base * 8
        other = d // 8 - partner_index * 8
        chosen = jnp.where((other >= 0) & (other < 8), 8 + other, 16)
        chosen = jnp.where((own >= 0) & (own < 8), own, chosen)
        og_in[128 * t:128 * t + 128, :] = cg_bank[chosen]
    for q in range(2):
        split = dot(og_in[...], p_unoct[:, 256 * q:256 * q + 256]).astype(BF)
        for t in range(8):
            for h in range(2):
                og_all[4 * t + 2 * q + h] = split[128 * t:128 * t + 128, 128 * h:128 * h + 128]
    for j in range(4):
        halves = []
        for h in range(2):
            t = 2 * j + h
            d = dest_s[0, t]
            octant = d - d // 8 * 8
            piece = og_all[4 * t + octant // 2].astype(F32)
            odd = octant - octant // 2 * 2
            halves.append(jnp.where(odd == h, piece, roll(piece, 64)))
        og[:, 128 * j:128 * j + 128] = jnp.where(low_half, halves[0], halves[1]).astype(BF)
    for r in range(4):
        rows = dot(wdt[128 * r:128 * r + 128, :], og[...]).astype(BF).astype(F32)
        for j in range(4):
            even = rows[0:64, 128 * j:128 * j + 128]
            odd = rows[64:128, 128 * j:128 * j + 128]
            columns = slice(128 * r, 128 * r + 128)
            ag_ph[128 * j:128 * j + 64, columns] = jnp.where(low64, even, roll(odd, 64)).astype(BF)
            ag_ph[128 * j + 64:128 * j + 128, columns] = jnp.where(
                low64, roll(even, 64), odd
            ).astype(BF)
    loads["unphase"].wait()
    for q in range(4):
        spread = dot(ag_ph[...], p_unphase[:, 256 * q:256 * q + 256]).astype(BF)
        for t in range(8):
            ag[t, :, 256 * q:256 * q + 256] = spread[64 * t:64 * t + 64]

    dest_send.wait_recv()
    dest_copy = pltpu.make_async_copy(dest_buf.at[1], dest_in, idx_sem.at[2])
    dest_copy.start()
    dest_copy.wait()
    place = lax.broadcasted_iota(jnp.int32, (8, 128), 1) + base * 64
    inverse = jnp.zeros((8, 128), jnp.int32) + 16
    for s in range(8):
        inverse = jnp.where(place == dest_s[0, s], s, inverse)
        inverse = jnp.where(place == dest_in[0, s], 8 + s, inverse)
    inv_v[...] = inverse
    inv_copy = pltpu.make_async_copy(inv_v, inv_s, idx_sem.at[3])
    inv_copy.start()

    loads["unpack"].wait()
    receive(bank1, 0, halo)

    def forward(r_buf, i, t, q):
        parts = convolve(wf, r_buf, i, q)
        for h in range(2):
            z = 2 * q + h
            v = parts[h]
            on = occ_p[t, :, 128 * z:128 * z + 128]
            s = 1.0 / (1.0 + jnp.exp(-v))
            act[t, :, 128 * z:128 * z + 128] = jnp.where(on > 0.5, v * s, 0.0).astype(BF)
            g = ag[t, :, 128 * z:128 * z + 128].astype(F32)
            g = g * s * (1.0 + v * (1.0 - s))
            pg[8 * t + z] = jnp.where(on > 0.5, g, 0.0).astype(BF)

    sweep(bank1, 0, 4, forward)

    wg[...] = jnp.zeros_like(wg)

    @pl.loop(0, 4)
    def _(i):
        for h in range(2):
            planes = [pg[8 * (2 * i + h) + z] for z in range(8)]
            shifted = jnp.concatenate(
                [
                    jnp.concatenate([roll(p, c - 1) for p in planes], axis=1)
                    for c in range(3)
                ],
                axis=0,
            )
            for a in range(3):
                wg[a] += dot_nt(shifted, (r0, r1)[h][i, :, 128 * a:128 * a + 1024])

    for a in range(3):
        src[192 * a:192 * a + 192, :] = wg[a, :, 0:128]
    src[576:768, :] = jnp.concatenate([wg[0, :, 128:192], wg[1, :, 128:192]], axis=1)
    src[768:960, 0:64] = wg[2, :, 128:192]
    src[768:960, 64:128] = jnp.zeros((192, 64), F32)
    src[960:1024, :] = jnp.zeros((64, 128), F32)


    def pair(n):
        return r_send.at[n], r_recv.at[n]

    def rows_at(start, size):
        return pl.ds(pl.multiple_of(start, 8), size)

    def axis_of(p, stage):
        return (p + stage) % 3

    def me(p, stage):
        return coordinate[axis_of(p, stage)]

    def first_row(p, half):
        return 512 * half + 256 * p if p < 2 else 1024 + 256 * half

    def stage_0(p, _):
        rows = rows_at(first_row(p, 1 - core), 256)
        return [send(src.at[rows], rc.at[p], *pair(p), partner)]

    def arrived(copies):
        for copy in copies:
            copy.wait_recv()

    def stage_1(p, before):
        arrived(before)
        s1[p] = src[rows_at(first_row(p, core), 256)] + rc[p]
        copies = []
        for d in (1, 2, 3):
            to = (me(p, 0) + d) % 4
            copies.append(
                send(
                    s1.at[p, rows_at(64 * to, 64)], t1.at[p, d - 1],
                    *pair(3 + 3 * p + d - 1), along(axis_of(p, 0), d),
                )
            )
        return copies

    def exchange(buffer, p, stage, value, first_pair):
        buffer[p, me(p, stage)] = value
        place = buffer.at[p, me(p, stage)]
        return [
            send(place, place, *pair(first_pair + 3 * p + d - 1), along(axis_of(p, stage), d))
            for d in (1, 2, 3)
        ]

    def stage_2(p, before):
        arrived(before)
        total = s1[p, rows_at(64 * me(p, 0), 64)]
        for d in range(3):
            total = total + t1[p, d]
        return exchange(t2, p, 1, total, 12)

    def stage_3(p, before):
        arrived(before)
        return exchange(t3, p, 2, (t2[p, 0] + t2[p, 1]) + (t2[p, 2] + t2[p, 3]), 21)

    def stage_4(p, before):
        arrived(before)
        rows = rows_at(first_row(p, core) + 64 * me(p, 0), 64)
        total = (t3[p, 0] + t3[p, 1]) + (t3[p, 2] + t3[p, 3])
        fin[rows] = (total * scale).astype(BF)
        return [
            send(fin.at[rows], fin.at[rows], *pair(30 + 3 * p + d - 1), along(axis_of(p, 0), d))
            for d in (1, 2, 3)
        ]

    def stage_5(p, before):
        arrived(before)
        rows = rows_at(first_row(p, core), 256)
        return [send(fin.at[rows], fin.at[rows], *pair(39 + p), partner)]

    stages = [stage_0, stage_1, stage_2, stage_3, stage_4, stage_5]
    reduced = [[], [], []]

    def reduce_step(*parts):
        for p in parts:
            n = len(reduced[p])
            reduced[p].append(stages[n](p, reduced[p][-1] if n > 0 else None))

    loads["phase"].wait()
    for q in range(2):
        split = dot(act[...].reshape(512, 1024), p_phase[:, 256 * q:256 * q + 256])
        for j in range(4):
            for h in range(2):
                even = split[128 * j:128 * j + 64, 128 * h:128 * h + 128]
                odd = split[128 * j + 64:128 * j + 128, 128 * h:128 * h + 128]
                k = 4 * q + 2 * h
                columns = slice(128 * j, 128 * j + 128)
                phases[64 * k:64 * k + 64, columns] = jnp.where(
                    low64, even, roll(odd, 64)
                ).astype(BF)
                phases[64 * k + 64:64 * k + 128, columns] = jnp.where(
                    low64, roll(even, 64), odd
                ).astype(BF)
    src[1024:1536, :] = dot_nt(phases[...], og[...])

    reduce_step(0, 1, 2)
    bl[...] = dot(wd[...], phases[...]).astype(BF)
    bl_send = send(bl, bl_in, c_send.at[2], c_recv.at[2], partner)

    loads["rewrap"].wait()
    for t in range(8):
        rows = pg[8 * t:8 * t + 8].reshape(512, 128)
        bank2[8 * t:8 * t + 8] = dot(rows, p_rewrap[...]).astype(BF).reshape(8, 64, 128)

    reduce_step(0, 1, 2)
    halo2 = publish(bank2, 1)

    inv_copy.wait()
    bl_send.wait_recv()
    bl_bank[16] = jnp.zeros((128, 128), BF)
    for source in range(2):
        blocks = (bl, bl_in)[source]
        for j in range(4):
            both = blocks[:, 128 * j:128 * j + 128].astype(F32)
            turned = roll(both, 64)
            bl_bank[8 * source + 2 * j] = jnp.where(low_half, both, turned).astype(BF)
            bl_bank[8 * source + 2 * j + 1] = jnp.where(low_half, turned, both).astype(BF)
    for c in range(8):
        for q in range(4):
            even = bl_bank[inv_s[0, 8 * c + 2 * q]]
            odd = bl_bank[inv_s[0, 8 * c + 2 * q + 1]]
            og_in[128 * c:128 * c + 128, 128 * q:128 * q + 128] = jnp.where(low_half, even, odd)
    loads["oct"].wait()
    for q in range(2):
        rows = dot(og_in[...], p_oct[:, 256 * q:256 * q + 256]).astype(BF)
        coarse_v[:, :, 256 * q:256 * q + 256] = rows.reshape(8, 128, 256)
    coarse_out = pltpu.make_async_copy(coarse_v, coarse, out_sem.at[1])
    coarse_out.start()
    reduce_step(0, 1, 2)
    receive(bank2, 1, halo2)
    reduce_step(0, 1, 2)

    def backward(r_buf, i, t, q):
        parts = convolve(wb, r_buf, i, q)
        for h in range(2):
            z = 2 * q + h
            on = occ_p[t, :, 128 * z:128 * z + 128]
            fg[t, :, 128 * z:128 * z + 128] = jnp.where(on > 0.5, parts[h], 0.0).astype(BF)

    sweep(bank2, 0, 2, backward)
    reduce_step(0, 1, 2)
    sweep(bank2, 2, 4, backward)
    reduce_step(0, 1, 2)
    loads["native"].wait()
    for q in range(4):
        rows = dot(fg[:, :, 256 * q:256 * q + 256].reshape(512, 256), p_native[...])
        feat_v[:, :, 128 * q:128 * q + 128] = rows.astype(BF).reshape(8, 64, 128)
    feat_out = pltpu.make_async_copy(feat_v, feat_grad, out_sem.at[0])
    feat_out.start()

    arrived(reduced[0][5] + reduced[1][5])
    for a in range(3):
        for c in range(3):
            for b in range(2):
                rows = slice(192 * a + 64 * c, 192 * a + 64 * c + 64)
                ws_v[9 * a + 3 * b + c] = fin[rows, 64 * b:64 * b + 64].astype(F32)
            row, column = ((576, 0), (576, 64), (768, 0))[a]
            rows = slice(row + 64 * c, row + 64 * c + 64)
            ws_v[9 * a + 6 + c] = fin[rows, column:column + 64].astype(F32)
    sub_out = pltpu.make_async_copy(ws_v, ws_out, out_sem.at[3])
    sub_out.start()
    arrived(reduced[2][5])
    wd_v[...] = fin[1024:1536, :].astype(F32)
    down_out = pltpu.make_async_copy(wd_v, wd_out, out_sem.at[2])
    down_out.start()
    for copy in halo + halo2 + [dest_send, cg_send, bl_send]:
        copy.wait_send()
    for stage in reduced:
        for copies in stage:
            for copy in copies:
                copy.wait_send()
    for copy in (feat_out, coarse_out, down_out, sub_out):
        copy.wait()


def write_out(*refs):
    sources, targets, sems = refs[:4], refs[4:8], refs[8]
    copies = [pltpu.make_async_copy(a, b, sems.at[n]) for n, (a, b) in enumerate(zip(sources, targets))]
    for copy in copies:
        copy.start()
    for copy in copies:
        copy.wait()


def shards(features, occupancy, neighbors, coarse_dest, w_sub, w_down, coarse_grad):
    devices = lax.axis_size("gz") * lax.axis_size("gy")
    scale = (features.shape[0] * devices * 512.0) ** -0.5
    anywhere = pl.BlockSpec(memory_space=pl.ANY)
    constants = permutations()
    vmem, smem, dma = pltpu.VMEM, pltpu.SMEM, pltpu.SemaphoreType.DMA
    i32 = jnp.int32
    held = pl.pallas_call(
        functools.partial(body, scale),
        out_shape=(
            vmem((8, 128, 512), BF), vmem((8, 64, 512), BF), vmem((27, 64, 64), F32), vmem((512, 128), F32),
        ),
        in_specs=[anywhere] * 16,
        out_specs=(anywhere,) * 4,
        scratch_shapes=[
            vmem((8, 27), i32), vmem((8, 512), i32), vmem((8, 64, 512), BF), vmem((1, 8), i32),
            smem((1, 8), i32), vmem((27, 64, 64), BF), vmem((8, 64, 128), BF),
        ] + [vmem(c.shape, BF) for c in constants] + [
            vmem((BANK, 64, 128), BF), vmem((BANK, 64, 128), BF),
            vmem((2, 2, 4, 64, 128), BF), vmem((2, 2, 4, 64, 128), BF), vmem((2, 2, 8, 64, 128), BF),
            vmem((2, 4, 64, 128), BF), vmem((2, 4, 64, 128), BF),
            vmem((8, 128), i32), smem((8, 128), i32), vmem((8, 128), i32), smem((8, 128), i32),
            vmem((2, 8, 128), i32), smem((8, 128), i32),
            vmem((17, 128, 512), BF), vmem((1024, 512), BF), vmem((32, 128, 128), BF),
            vmem((128, 512), BF), vmem((512, 512), BF), vmem((8, 64, 1024), BF),
            vmem((8, 1, 1024), F32), vmem((5, 192, 1280), BF), vmem((4, 192, 1280), BF),
            vmem((8, 64, 1024), BF), vmem((512, 512), BF), vmem((64, 64, 128), BF),
            vmem((3, 192, 192), BF), vmem((3, 192, 192), BF), vmem((128, 512), BF), vmem((512, 128), BF),
            vmem((128, 512), BF), vmem((128, 512), BF), vmem((17, 128, 128), BF),
            vmem((8, 64, 1024), BF), vmem((3, 192, 192), F32),
            vmem((8, 128, 512), BF), vmem((8, 64, 512), BF), vmem((27, 64, 64), F32),
            vmem((1536, 128), F32), vmem((3, 256, 128), F32), vmem((3, 256, 128), F32),
            vmem((3, 3, 64, 128), F32), vmem((3, 4, 64, 128), F32), vmem((3, 4, 64, 128), F32),
            vmem((1536, 128), BF), vmem((512, 128), F32),
            dma((2, 8)), dma((2, 8)), dma((3,)), dma((3,)), dma((18,)), dma((4,)), dma((4,)),
            dma((42,)), dma((42,)),
        ],
        compiler_params=pltpu.CompilerParams(
            collective_id=0, has_side_effects=True, vmem_limit_bytes=60 * 1024 * 1024
        ),
        cost_estimate=pl.CostEstimate(flops=6 * 10**9, bytes_accessed=12 * 10**6, transcendentals=10**6),
        name="sparse_conv",
    )(
        neighbors, occupancy, features, coarse_dest.reshape(1, 8), w_sub,
        w_down.transpose(0, 2, 1), coarse_grad, *constants,
    )
    coarse, feat_grad, ws, wd = pl.pallas_call(
        write_out,
        out_shape=[jax.ShapeDtypeStruct(x.shape, x.dtype) for x in held],
        in_specs=[anywhere] * 4,
        out_specs=[anywhere] * 4,
        scratch_shapes=[dma((4,))],
        compiler_params=pltpu.CompilerParams(vmem_limit_bytes=1024 * 1024),
        name="write_out",
    )(*held)
    return coarse, feat_grad, ws, wd.reshape(8, 64, 128).transpose(0, 2, 1)


def solution(mesh):
    return jax.shard_map(
        shards,
        mesh=mesh,
        in_specs=(
            P(("gz", "gy"), None, None),
            P(("gz", "gy"), None),
            P(("gz", "gy"), None),
            P(("gz", "gy")),
            P(),
            P(),
            P(("gz", "gy"), None, None),
        ),
        out_specs=(P(("gz", "gy"), None, None), P(("gz", "gy"), None, None), P(), P()),
        check_vma=False,
    )
```

```python
import functools

import jax
import jax.numpy as jnp
import numpy as np
from jax import lax
from jax.experimental import pallas as pl
from jax.experimental.pallas import tpu as pltpu
from jax.sharding import PartitionSpec as P

MESH = pl.DeviceIdType.MESH
BF = jnp.bfloat16
F32 = jnp.float32

Y_SIDES, ZERO, Z_LOW, Z_HIGH, DIAGONAL, BANK = 64, 128, 136, 144, 152, 168


def one_hot(shape, pairs):
    out = np.zeros(shape, np.float32)
    for row, column in pairs:
        out[row, column] = 1.0
    return jnp.asarray(out, BF)


def lane(y, x):
    return 10 * (y + 1) + x + 1


def permutations():
    wrap = [
        (64 * h + 8 * ((yp - 1) % 8) + (xp - 1) % 8, 128 * h + 10 * yp + xp)
        for h in range(2) for yp in range(10) for xp in range(10)
    ]
    rewrap = [
        (lane((yp - 1) % 8, (xp - 1) % 8), 10 * yp + xp) for yp in range(10) for xp in range(10)
    ]
    native = [
        (128 * h + lane(y, x), 64 * h + 8 * y + x)
        for h in range(2) for y in range(8) for x in range(8)
    ]
    pack = [
        (128 * z + 90 * side + x + 1, 64 * side + 8 * z + x)
        for side in range(2) for z in range(8) for x in range(8)
    ]
    unpack = [
        (128 * side + 64 * parity + 8 * z + (xp - 1) % 8, 1024 * parity + 128 * z + 90 * side + xp)
        for side in range(2) for parity in range(2) for z in range(8) for xp in range(10)
    ]
    phase, octant = [], []
    for z in range(8):
        for y in range(8):
            for x in range(8):
                k = 4 * (z % 2) + 2 * (y % 2) + x % 2
                v = 16 * (z // 2) + 4 * (y // 2) + x // 2
                phase.append((128 * z + lane(y, x), 64 * k + v))
                k = 4 * (z // 4) + 2 * (y // 4) + x // 4
                v = 16 * (z % 4) + 4 * (y % 4) + x % 4
                octant.append((64 * k + v, 64 * z + 8 * y + x))
    flip = lambda pairs: [(b, a) for a, b in pairs]
    return (
        one_hot((128, 256), wrap),
        one_hot((128, 128), rewrap),
        one_hot((256, 128), native),
        one_hot((1024, 128), pack),
        one_hot((256, 2048), unpack),
        one_hot((1024, 512), phase),
        one_hot((512, 1024), flip(phase)),
        one_hot((512, 512), octant),
        one_hot((512, 512), flip(octant)),
    )


def dot(a, b):
    return jnp.dot(a, b, preferred_element_type=F32)


def dot_nt(a, b):
    return lax.dot_general(a, b, (((1,), (1,)), ((), ())), preferred_element_type=F32)


def roll(x, shift):
    return pltpu.roll(x, shift % 128, x.ndim - 1)


PERMUTATIONS = ("wrap", "rewrap", "native", "pack", "unpack", "phase", "unphase", "oct", "unoct")


def body(scale, *refs):
    operands, results, scratch = refs[:16], refs[16:20], refs[20:]
    nbr_h, occ_h, feat_h, dest_h, w_sub_h, w_down_h, cgrad = operands[:7]
    coarse, feat_grad, ws_out, wd_out = results
    nbr, occ, feat, dest_v, dest_s, w_sub, w_down = scratch[:7]
    p_wrap, p_rewrap, p_native, p_pack, p_unpack, p_phase, p_unphase, p_oct, p_unoct = scratch[7:16]
    (
        bank1, bank2, ysend, ydst, zsend, dsend, drecv, idx_v, idx_s, inv_v, inv_s, dest_buf, dest_in,
        cg_bank, og_in, og_all, og, ag_ph, ag, occ_p, r0, r1, act, phases, pg, wf, wb, wd, wdt,
        bl, bl_in, bl_bank, fg, wg, coarse_v, feat_v, ws_v,
        src, rc, s1, t1, t2, t3, fin, wd_v,
        h_send, h_recv, c_send, c_recv, in_sem, idx_sem, out_sem, r_send, r_recv,
    ) = scratch[16:]
    gz, gy = lax.axis_index("gz"), lax.axis_index("gy")
    cy, cz, core = gz // 8, (gz // 2) % 4, gz % 2
    nz, ny = 32, 4

    def at(dz, dy):
        return {"gz": (gz + dz + nz) % nz, "gy": (gy + dy + ny) % ny}

    def along(axis, d):
        if axis == 0:
            return {"gz": gz, "gy": (gy + d) % 4}
        if axis == 1:
            return {"gz": ((cy + d) % 4 * 4 + cz) * 2 + core, "gy": gy}
        return {"gz": (cy * 4 + (cz + d) % 4) * 2 + core, "gy": gy}

    coordinate = (gy, cy, cz)
    partner = {"gz": gz + 1 - 2 * core, "gy": gy}
    halo_steps = [(dz, dy) for dz in (-1, 0, 1) for dy in (-1, 0, 1) if (dz, dy) != (0, 0)]
    barrier = pltpu.get_barrier_semaphore()
    greeted = [at(*s) for s in halo_steps] + [partner]
    greeted += [along(axis, d) for axis in range(3) for d in (1, 2, 3)]
    for device in greeted:
        pl.semaphore_signal(barrier, inc=1, device_id=device, device_id_type=MESH)

    loads = {}

    def load(name, source, target):
        loads[name] = pltpu.make_async_copy(source, target, in_sem.at[len(loads)])
        loads[name].start()

    permuting = dict(zip(PERMUTATIONS, zip(operands[7:], scratch[7:16])))
    load("feat", feat_h, feat)
    load("occ", occ_h, occ)
    load("wrap", *permuting["wrap"])
    load("nbr", nbr_h, nbr)
    load("dest", dest_h, dest_v)
    load("dest_s", dest_h, dest_s)
    load("pack", *permuting["pack"])
    load("w_sub", w_sub_h, w_sub)
    load("w_down", w_down_h, w_down)
    load("cgrad", cgrad, cg_bank.at[pl.ds(0, 8)])
    for name in ("unoct", "unphase", "unpack", "rewrap", "phase", "native", "oct"):
        load(name, *permuting[name])

    def send(src, dst, send_sem, recv_sem, device):
        copy = pltpu.make_async_remote_copy(
            src_ref=src, dst_ref=dst, send_sem=send_sem, recv_sem=recv_sem,
            device_id=device, device_id_type=MESH,
        )
        copy.start()
        return copy

    lanes = lax.broadcasted_iota(jnp.int32, (64, 128), 1)
    low_half = lax.broadcasted_iota(jnp.int32, (128, 128), 1) < 64
    xp = lanes - 10 * lax.shift_right_logical(lanes * 205, 11)
    first, last = xp == 0, xp == 9
    low64 = lanes < 64
    yp_low, yp_high = lanes < 10, lanes >= 90
    center_row = lax.broadcasted_iota(jnp.int32, (8, 128), 1)
    center_x = center_row - 10 * lax.shift_right_logical(center_row * 205, 11)
    center = (center_row > 10) & (center_row < 89) & (center_x > 0) & (center_x < 9)

    loads["nbr"].wait()
    table = nbr[...]
    owner = table // 8
    slot = table - owner * 8
    step_z = owner // 4 - gz
    step_y = owner - owner // 4 * 4 - gy
    column = lax.broadcasted_iota(jnp.int32, (8, 27), 1)
    part_a = column // 9
    edge_z = jnp.where(part_a == 0, 7, 0)
    on_z = Z_LOW + jnp.where(step_z > 0, 8, 0) + slot
    on_diagonal = DIAGONAL + jnp.where(step_z > 0, 8, 0) + slot
    same_z = jnp.where(step_y == 0, 0, Y_SIDES) + slot * 8 + edge_z
    index = jnp.where(step_z == 0, same_z, jnp.where(step_y == 0, on_z, on_diagonal))
    index = jnp.where((table < 0) | ((part_a == 1) & (index > ZERO)), ZERO, index)
    idx_v[...] = jnp.zeros_like(idx_v)
    idx_v[:, 0:27] = index
    idx_copy = pltpu.make_async_copy(idx_v, idx_s, idx_sem.at[0])
    idx_copy.start()

    loads["feat"].wait()
    loads["occ"].wait()
    loads["wrap"].wait()
    for q in range(4):
        part = feat[:, :, 128 * q:128 * q + 128]
        flag = occ[:, 128 * q:128 * q + 128].astype(F32).astype(BF)
        rows = [part[t] * flag[t:t + 1] for t in range(8)]
        planes = dot(jnp.concatenate(rows, axis=0), p_wrap[...]).astype(BF)
        flags = dot(flag, p_wrap[...])
        for h in range(2):
            flag_plane = jnp.where(center, flags[:, 128 * h:128 * h + 128], 0.0)
            for t in range(8):
                occ_p[t, :, 128 * (2 * q + h):128 * (2 * q + h) + 128] = flag_plane[t:t + 1]
                bank1[8 * t + 2 * q + h] = planes[64 * t:64 * t + 64, 128 * h:128 * h + 128]

    loads["dest"].wait()
    dest_buf[0] = jnp.zeros((8, 128), jnp.int32) - 1
    dest_buf[0, 0:1, 0:8] = dest_v[...]
    for bank in (bank1, bank2):
        bank[ZERO:ZERO + 8] = jnp.zeros((8, 64, 128), BF)
    loads["pack"].wait()

    pl.semaphore_wait(barrier, len(greeted))
    dest_send = send(dest_buf.at[0], dest_buf.at[1], c_send.at[0], c_recv.at[0], partner)
    cg_send = send(cgrad, cg_bank.at[pl.ds(8, 8)], c_send.at[1], c_recv.at[1], partner)

    def publish(bank, which):
        copies = []
        total = None
        for q in range(4):
            both = jnp.concatenate(
                [
                    jnp.concatenate([bank[8 * t + 2 * q], bank[8 * t + 2 * q + 1]], axis=1)
                    for t in range(8)
                ],
                axis=0,
            )
            term = dot(both, p_pack[256 * q:256 * q + 256, :])
            total = term if total is None else total + term
        for j in range(4):
            even, odd = total[128 * j:128 * j + 64], total[128 * j + 64:128 * j + 128]
            ysend[which, 0, j] = jnp.where(low64, even, roll(odd, 64)).astype(BF)
            ysend[which, 1, j] = jnp.where(low64, roll(even, 64), odd).astype(BF)
        for side in range(2):
            for t in range(8):
                zsend[which, side, t] = bank[8 * t + (7 if side == 0 else 0)]
        for side in range(2):
            up = 1 - 2 * side
            copies.append(
                send(
                    ysend.at[which, side], ydst.at[which, side],
                    h_send.at[which, side], h_recv.at[which, side], at(0, up),
                )
            )
            copies.append(
                send(
                    zsend.at[which, side], bank.at[pl.ds(Z_LOW if side == 0 else Z_HIGH, 8)],
                    h_send.at[which, 2 + side], h_recv.at[which, 2 + side], at(up, 0),
                )
            )
        for side_z in range(2):
            for side_y in range(2):
                number = 2 * side_z + side_y
                gathered = jnp.zeros((64, 128), BF)
                for t in range(8):
                    piece = roll(bank[8 * t + (7 if side_z == 0 else 0)], 16 * t - 90 * side_y)
                    inside = (lanes >= 16 * t) & (lanes < 16 * t + 10)
                    gathered = jnp.where(inside, piece, gathered)
                dsend[which, number] = gathered
                copies.append(
                    send(
                        dsend.at[which, number], drecv.at[which, number],
                        h_send.at[which, 4 + number], h_recv.at[which, 4 + number],
                        at(1 - 2 * side_z, 1 - 2 * side_y),
                    )
                )
        return copies

    def receive(bank, which, copies):
        for copy in copies:
            copy.wait_recv()
        rows = jnp.concatenate([ydst[which, side].reshape(256, 128) for side in range(2)], axis=1)
        for q in range(8):
            planes = dot(rows, p_unpack[:, 256 * q:256 * q + 256]).astype(BF)
            for j in range(4):
                for h in range(2):
                    t, z = 2 * j + q // 4, 2 * (q % 4) + h
                    bank[Y_SIDES + 8 * t + z] = planes[64 * j:64 * j + 64, 128 * h:128 * h + 128]
        for side_z in range(2):
            below, above = drecv[which, 2 * side_z], drecv[which, 2 * side_z + 1]
            for t in range(8):
                bank[DIAGONAL + 8 * side_z + t] = jnp.where(
                    yp_low, roll(below, -16 * t), roll(above, 90 - 16 * t)
                )

    def assemble(bank, t, r_buf, i, planes):
        for zp in planes:
            a = 0 if zp == 0 else (2 if zp == 9 else 1)
            rows = []
            for b in range(3):
                loaded = []
                for c in range(3):
                    place = idx_s[t, 9 * a + 3 * b + c] + (zp - 1 if a == 1 else 0)
                    loaded.append(bank[place])
                rows.append(jnp.where(first, loaded[0], jnp.where(last, loaded[2], loaded[1])))
            plane = jnp.where(yp_low, rows[0], jnp.where(yp_high, rows[2], rows[1]))
            wide = plane.astype(F32)
            columns = slice(128 * zp, 128 * zp + 128)
            r_buf[i, 0:64, columns] = roll(wide, 10).astype(BF)
            r_buf[i, 64:128, columns] = plane
            r_buf[i, 128:192, columns] = roll(wide, -10).astype(BF)

    def convolve(weights, r_buf, i, q):
        total = None
        for a in range(3):
            term = dot(weights[a], r_buf[i, :, 128 * a + 256 * q:128 * a + 256 * q + 256])
            total = term if total is None else total + term
        parts = []
        for h in range(2):
            y = total[:, 128 * h:128 * h + 128]
            parts.append(roll(y[0:64], 1) + y[64:128] + roll(y[128:192], -1))
        return parts

    groups = ((0, 1, 2), (3, 4, 5), (6, 7), (8, 9))

    def sweep(bank, low, high, tile):
        if low == 0:
            for planes in groups:
                assemble(bank, 0, r0, 0, planes)

        @pl.loop(low, high)
        def _(i):
            for q in range(4):
                assemble(bank, 2 * i + 1, r1, i, groups[q])
                tile(r0, i, 2 * i, q)
            for q in range(4):
                assemble(bank, jnp.minimum(2 * i + 2, 7), r0, i + 1, groups[q])
                tile(r1, i, 2 * i + 1, q)

    halo = publish(bank1, 0)

    loads["w_sub"].wait()
    loads["w_down"].wait()
    for a in range(3):
        for c in range(3):
            wf[a, 64 * c:64 * c + 64, :] = jnp.concatenate(
                [w_sub[9 * a + 3 * b + c].astype(F32) for b in range(3)], axis=1
            ).astype(BF)
        turned = jnp.concatenate(
            [
                jnp.concatenate(
                    [w_sub[9 * (2 - a) + 3 * (2 - b) + 2 - c].astype(F32) for c in range(3)], axis=1
                )
                for b in range(3)
            ],
            axis=0,
        )
        wb[a] = turned.T.astype(BF)
    wdt[...] = w_down[...].reshape(512, 128)
    wd[...] = wdt[...].astype(F32).T.astype(BF)

    cg_bank[16] = jnp.zeros((128, 512), BF)
    idx_copy.wait()
    loads["dest_s"].wait()
    loads["cgrad"].wait()
    loads["unoct"].wait()
    cg_send.wait_recv()
    base = gz * 4 + gy
    partner_index = (gz + 1 - 2 * core) * 4 + gy
    for t in range(8):
        d = dest_s[0, t]
        own = d // 8 - base * 8
        other = d // 8 - partner_index * 8
        chosen = jnp.where((other >= 0) & (other < 8), 8 + other, 16)
        chosen = jnp.where((own >= 0) & (own < 8), own, chosen)
        og_in[128 * t:128 * t + 128, :] = cg_bank[chosen]
    for q in range(2):
        split = dot(og_in[...], p_unoct[:, 256 * q:256 * q + 256]).astype(BF)
        for t in range(8):
            for h in range(2):
                og_all[4 * t + 2 * q + h] = split[128 * t:128 * t + 128, 128 * h:128 * h + 128]
    for j in range(4):
        halves = []
        for h in range(2):
            t = 2 * j + h
            d = dest_s[0, t]
            octant = d - d // 8 * 8
            piece = og_all[4 * t + octant // 2].astype(F32)
            odd = octant - octant // 2 * 2
            halves.append(jnp.where(odd == h, piece, roll(piece, 64)))
        og[:, 128 * j:128 * j + 128] = jnp.where(low_half, halves[0], halves[1]).astype(BF)
    for r in range(4):
        rows = dot(wdt[128 * r:128 * r + 128, :], og[...]).astype(BF).astype(F32)
        for j in range(4):
            even = rows[0:64, 128 * j:128 * j + 128]
            odd = rows[64:128, 128 * j:128 * j + 128]
            columns = slice(128 * r, 128 * r + 128)
            ag_ph[128 * j:128 * j + 64, columns] = jnp.where(low64, even, roll(odd, 64)).astype(BF)
            ag_ph[128 * j + 64:128 * j + 128, columns] = jnp.where(
                low64, roll(even, 64), odd
            ).astype(BF)
    loads["unphase"].wait()
    for q in range(4):
        spread = dot(ag_ph[...], p_unphase[:, 256 * q:256 * q + 256]).astype(BF)
        for t in range(8):
            ag[t, :, 256 * q:256 * q + 256] = spread[64 * t:64 * t + 64]

    dest_send.wait_recv()
    dest_copy = pltpu.make_async_copy(dest_buf.at[1], dest_in, idx_sem.at[2])
    dest_copy.start()
    dest_copy.wait()
    place = lax.broadcasted_iota(jnp.int32, (8, 128), 1) + base * 64
    inverse = jnp.zeros((8, 128), jnp.int32) + 16
    for s in range(8):
        inverse = jnp.where(place == dest_s[0, s], s, inverse)
        inverse = jnp.where(place == dest_in[0, s], 8 + s, inverse)
    inv_v[...] = inverse
    inv_copy = pltpu.make_async_copy(inv_v, inv_s, idx_sem.at[3])
    inv_copy.start()

    loads["unpack"].wait()
    receive(bank1, 0, halo)

    def forward(r_buf, i, t, q):
        parts = convolve(wf, r_buf, i, q)
        for h in range(2):
            z = 2 * q + h
            v = parts[h]
            on = occ_p[t, :, 128 * z:128 * z + 128]
            s = 1.0 / (1.0 + jnp.exp(-v))
            act[t, :, 128 * z:128 * z + 128] = jnp.where(on > 0.5, v * s, 0.0).astype(BF)
            g = ag[t, :, 128 * z:128 * z + 128].astype(F32)
            g = g * s * (1.0 + v * (1.0 - s))
            pg[8 * t + z] = jnp.where(on > 0.5, g, 0.0).astype(BF)

    sweep(bank1, 0, 4, forward)

    wg[...] = jnp.zeros_like(wg)

    @pl.loop(0, 4)
    def _(i):
        for h in range(2):
            planes = [pg[8 * (2 * i + h) + z] for z in range(8)]
            shifted = jnp.concatenate(
                [
                    jnp.concatenate([roll(p, c - 1) for p in planes], axis=1)
                    for c in range(3)
                ],
                axis=0,
            )
            for a in range(3):
                wg[a] += dot_nt(shifted, (r0, r1)[h][i, :, 128 * a:128 * a + 1024])

    for a in range(3):
        src[192 * a:192 * a + 192, :] = wg[a, :, 0:128]
    src[576:768, :] = jnp.concatenate([wg[0, :, 128:192], wg[1, :, 128:192]], axis=1)
    src[768:960, 0:64] = wg[2, :, 128:192]
    src[768:960, 64:128] = jnp.zeros((192, 64), F32)
    src[960:1024, :] = jnp.zeros((64, 128), F32)


    def pair(n):
        return r_send.at[n], r_recv.at[n]

    def rows_at(start, size):
        return pl.ds(pl.multiple_of(start, 8), size)

    def axis_of(p, stage):
        return (p + stage) % 3

    def me(p, stage):
        return coordinate[axis_of(p, stage)]

    def first_row(p, half):
        return 512 * half + 256 * p if p < 2 else 1024 + 256 * half

    def stage_0(p, _):
        rows = rows_at(first_row(p, 1 - core), 256)
        return [send(src.at[rows], rc.at[p], *pair(p), partner)]

    def arrived(copies):
        for copy in copies:
            copy.wait_recv()

    def stage_1(p, before):
        arrived(before)
        s1[p] = src[rows_at(first_row(p, core), 256)] + rc[p]
        copies = []
        for d in (1, 2, 3):
            to = (me(p, 0) + d) % 4
            copies.append(
                send(
                    s1.at[p, rows_at(64 * to, 64)], t1.at[p, d - 1],
                    *pair(3 + 3 * p + d - 1), along(axis_of(p, 0), d),
                )
            )
        return copies

    def exchange(buffer, p, stage, value, first_pair):
        buffer[p, me(p, stage)] = value
        place = buffer.at[p, me(p, stage)]
        return [
            send(place, place, *pair(first_pair + 3 * p + d - 1), along(axis_of(p, stage), d))
            for d in (1, 2, 3)
        ]

    def stage_2(p, before):
        arrived(before)
        total = s1[p, rows_at(64 * me(p, 0), 64)]
        for d in range(3):
            total = total + t1[p, d]
        return exchange(t2, p, 1, total, 12)

    def stage_3(p, before):
        arrived(before)
        return exchange(t3, p, 2, (t2[p, 0] + t2[p, 1]) + (t2[p, 2] + t2[p, 3]), 21)

    def stage_4(p, before):
        arrived(before)
        rows = rows_at(first_row(p, core) + 64 * me(p, 0), 64)
        total = (t3[p, 0] + t3[p, 1]) + (t3[p, 2] + t3[p, 3])
        fin[rows] = (total * scale).astype(BF)
        return [
            send(fin.at[rows], fin.at[rows], *pair(30 + 3 * p + d - 1), along(axis_of(p, 0), d))
            for d in (1, 2, 3)
        ]

    def stage_5(p, before):
        arrived(before)
        rows = rows_at(first_row(p, core), 256)
        return [send(fin.at[rows], fin.at[rows], *pair(39 + p), partner)]

    stages = [stage_0, stage_1, stage_2, stage_3, stage_4, stage_5]
    reduced = [[], [], []]

    def reduce_step(*parts):
        for p in parts:
            n = len(reduced[p])
            reduced[p].append(stages[n](p, reduced[p][-1] if n > 0 else None))

    loads["phase"].wait()
    for q in range(2):
        split = dot(act[...].reshape(512, 1024), p_phase[:, 256 * q:256 * q + 256]).astype(BF)
        for j in range(4):
            for h in range(2):
                even = split[128 * j:128 * j + 64, 128 * h:128 * h + 128]
                odd = split[128 * j + 64:128 * j + 128, 128 * h:128 * h + 128]
                k = 4 * q + 2 * h
                columns = slice(128 * j, 128 * j + 128)
                phases[64 * k:64 * k + 64, columns] = jnp.where(low64, even, roll(odd, 64))
                phases[64 * k + 64:64 * k + 128, columns] = jnp.where(low64, roll(even, 64), odd)
    src[1024:1536, :] = dot_nt(phases[...], og[...])

    reduce_step(0, 1, 2)
    bl[...] = dot(wd[...], phases[...]).astype(BF)
    bl_send = send(bl, bl_in, c_send.at[2], c_recv.at[2], partner)

    loads["rewrap"].wait()
    for t in range(8):
        rows = pg[8 * t:8 * t + 8].reshape(512, 128)
        bank2[8 * t:8 * t + 8] = dot(rows, p_rewrap[...]).astype(BF).reshape(8, 64, 128)

    reduce_step(0, 1, 2)
    halo2 = publish(bank2, 1)

    inv_copy.wait()
    bl_send.wait_recv()
    bl_bank[16] = jnp.zeros((128, 128), BF)
    for source in range(2):
        blocks = (bl, bl_in)[source]
        for j in range(4):
            both = blocks[:, 128 * j:128 * j + 128].astype(F32)
            turned = roll(both, 64)
            bl_bank[8 * source + 2 * j] = jnp.where(low_half, both, turned).astype(BF)
            bl_bank[8 * source + 2 * j + 1] = jnp.where(low_half, turned, both).astype(BF)
    for c in range(8):
        for q in range(4):
            even = bl_bank[inv_s[0, 8 * c + 2 * q]]
            odd = bl_bank[inv_s[0, 8 * c + 2 * q + 1]]
            og_in[128 * c:128 * c + 128, 128 * q:128 * q + 128] = jnp.where(low_half, even, odd)
    loads["oct"].wait()
    for q in range(2):
        rows = dot(og_in[...], p_oct[:, 256 * q:256 * q + 256]).astype(BF)
        coarse_v[:, :, 256 * q:256 * q + 256] = rows.reshape(8, 128, 256)
    coarse_out = pltpu.make_async_copy(coarse_v, coarse, out_sem.at[1])
    coarse_out.start()
    reduce_step(0, 1, 2)
    receive(bank2, 1, halo2)
    reduce_step(0, 1, 2)

    def backward(r_buf, i, t, q):
        parts = convolve(wb, r_buf, i, q)
        for h in range(2):
            z = 2 * q + h
            on = occ_p[t, :, 128 * z:128 * z + 128]
            fg[t, :, 128 * z:128 * z + 128] = jnp.where(on > 0.5, parts[h], 0.0).astype(BF)

    sweep(bank2, 0, 2, backward)
    reduce_step(0, 1, 2)
    sweep(bank2, 2, 4, backward)
    reduce_step(0, 1, 2)
    loads["native"].wait()
    for q in range(4):
        rows = dot(fg[:, :, 256 * q:256 * q + 256].reshape(512, 256), p_native[...])
        feat_v[:, :, 128 * q:128 * q + 128] = rows.astype(BF).reshape(8, 64, 128)
    feat_out = pltpu.make_async_copy(feat_v, feat_grad, out_sem.at[0])
    feat_out.start()

    arrived(reduced[0][5] + reduced[1][5])
    for a in range(3):
        for c in range(3):
            for b in range(2):
                rows = slice(192 * a + 64 * c, 192 * a + 64 * c + 64)
                ws_v[9 * a + 3 * b + c] = fin[rows, 64 * b:64 * b + 64].astype(F32)
            row, column = ((576, 0), (576, 64), (768, 0))[a]
            rows = slice(row + 64 * c, row + 64 * c + 64)
            ws_v[9 * a + 6 + c] = fin[rows, column:column + 64].astype(F32)
    sub_out = pltpu.make_async_copy(ws_v, ws_out, out_sem.at[3])
    sub_out.start()
    arrived(reduced[2][5])
    wd_v[...] = fin[1024:1536, :].astype(F32)
    down_out = pltpu.make_async_copy(wd_v, wd_out, out_sem.at[2])
    down_out.start()
    for copy in halo + halo2 + [dest_send, cg_send, bl_send]:
        copy.wait_send()
    for stage in reduced:
        for copies in stage:
            for copy in copies:
                copy.wait_send()
    for copy in (feat_out, coarse_out, down_out, sub_out):
        copy.wait()


def write_out(*refs):
    sources, targets, sems = refs[:4], refs[4:8], refs[8]
    copies = [pltpu.make_async_copy(a, b, sems.at[n]) for n, (a, b) in enumerate(zip(sources, targets))]
    for copy in copies:
        copy.start()
    for copy in copies:
        copy.wait()


def shards(features, occupancy, neighbors, coarse_dest, w_sub, w_down, coarse_grad):
    devices = lax.axis_size("gz") * lax.axis_size("gy")
    scale = (features.shape[0] * devices * 512.0) ** -0.5
    anywhere = pl.BlockSpec(memory_space=pl.ANY)
    constants = permutations()
    vmem, smem, dma = pltpu.VMEM, pltpu.SMEM, pltpu.SemaphoreType.DMA
    i32 = jnp.int32
    held = pl.pallas_call(
        functools.partial(body, scale),
        out_shape=(
            vmem((8, 128, 512), BF), vmem((8, 64, 512), BF), vmem((27, 64, 64), F32), vmem((512, 128), F32),
        ),
        in_specs=[anywhere] * 16,
        out_specs=(anywhere,) * 4,
        scratch_shapes=[
            vmem((8, 27), i32), vmem((8, 512), i32), vmem((8, 64, 512), BF), vmem((1, 8), i32),
            smem((1, 8), i32), vmem((27, 64, 64), BF), vmem((8, 64, 128), BF),
        ] + [vmem(c.shape, BF) for c in constants] + [
            vmem((BANK, 64, 128), BF), vmem((BANK, 64, 128), BF),
            vmem((2, 2, 4, 64, 128), BF), vmem((2, 2, 4, 64, 128), BF), vmem((2, 2, 8, 64, 128), BF),
            vmem((2, 4, 64, 128), BF), vmem((2, 4, 64, 128), BF),
            vmem((8, 128), i32), smem((8, 128), i32), vmem((8, 128), i32), smem((8, 128), i32),
            vmem((2, 8, 128), i32), smem((8, 128), i32),
            vmem((17, 128, 512), BF), vmem((1024, 512), BF), vmem((32, 128, 128), BF),
            vmem((128, 512), BF), vmem((512, 512), BF), vmem((8, 64, 1024), BF),
            vmem((8, 1, 1024), F32), vmem((5, 192, 1280), BF), vmem((4, 192, 1280), BF),
            vmem((8, 64, 1024), BF), vmem((512, 512), BF), vmem((64, 64, 128), BF),
            vmem((3, 192, 192), BF), vmem((3, 192, 192), BF), vmem((128, 512), BF), vmem((512, 128), BF),
            vmem((128, 512), BF), vmem((128, 512), BF), vmem((17, 128, 128), BF),
            vmem((8, 64, 1024), BF), vmem((3, 192, 192), F32),
            vmem((8, 128, 512), BF), vmem((8, 64, 512), BF), vmem((27, 64, 64), F32),
            vmem((1536, 128), F32), vmem((3, 256, 128), F32), vmem((3, 256, 128), F32),
            vmem((3, 3, 64, 128), F32), vmem((3, 4, 64, 128), F32), vmem((3, 4, 64, 128), F32),
            vmem((1536, 128), BF), vmem((512, 128), F32),
            dma((2, 8)), dma((2, 8)), dma((3,)), dma((3,)), dma((18,)), dma((4,)), dma((4,)),
            dma((42,)), dma((42,)),
        ],
        compiler_params=pltpu.CompilerParams(
            collective_id=0, has_side_effects=True, vmem_limit_bytes=60 * 1024 * 1024
        ),
        cost_estimate=pl.CostEstimate(flops=6 * 10**9, bytes_accessed=12 * 10**6, transcendentals=10**6),
        name="sparse_conv",
    )(
        neighbors, occupancy, features, coarse_dest.reshape(1, 8), w_sub,
        w_down.transpose(0, 2, 1), coarse_grad, *constants,
    )
    coarse, feat_grad, ws, wd = pl.pallas_call(
        write_out,
        out_shape=[jax.ShapeDtypeStruct(x.shape, x.dtype) for x in held],
        in_specs=[anywhere] * 4,
        out_specs=[anywhere] * 4,
        scratch_shapes=[dma((4,))],
        compiler_params=pltpu.CompilerParams(vmem_limit_bytes=1024 * 1024),
        name="write_out",
    )(*held)
    return coarse, feat_grad, ws, wd.reshape(8, 64, 128).transpose(0, 2, 1)


def solution(mesh):
    return jax.shard_map(
        shards,
        mesh=mesh,
        in_specs=(
            P(("gz", "gy"), None, None),
            P(("gz", "gy"), None),
            P(("gz", "gy"), None),
            P(("gz", "gy")),
            P(),
            P(),
            P(("gz", "gy"), None, None),
        ),
        out_specs=(P(("gz", "gy"), None, None), P(("gz", "gy"), None, None), P(), P()),
        check_vma=False,
    )
```

```python
import functools

import jax
import jax.numpy as jnp
import numpy as np
from jax import lax
from jax.experimental import pallas as pl
from jax.experimental.pallas import tpu as pltpu
from jax.sharding import PartitionSpec as P

MESH = pl.DeviceIdType.MESH
BF = jnp.bfloat16
F32 = jnp.float32

Y_SIDES, ZERO, Z_LOW, Z_HIGH, DIAGONAL, BANK = 64, 128, 136, 144, 152, 168


def one_hot(shape, pairs):
    out = np.zeros(shape, np.float32)
    for row, column in pairs:
        out[row, column] = 1.0
    return jnp.asarray(out, BF)


def lane(y, x):
    return 10 * (y + 1) + x + 1


def permutations():
    wrap = [
        (64 * h + 8 * ((yp - 1) % 8) + (xp - 1) % 8, 128 * h + 10 * yp + xp)
        for h in range(2) for yp in range(10) for xp in range(10)
    ]
    rewrap = [
        (lane((yp - 1) % 8, (xp - 1) % 8), 10 * yp + xp) for yp in range(10) for xp in range(10)
    ]
    native = [
        (128 * h + lane(y, x), 64 * h + 8 * y + x)
        for h in range(2) for y in range(8) for x in range(8)
    ]
    pack = [
        (128 * z + 90 * side + x + 1, 64 * side + 8 * z + x)
        for side in range(2) for z in range(8) for x in range(8)
    ]
    unpack = [
        (128 * side + 64 * parity + 8 * z + (xp - 1) % 8, 1024 * parity + 128 * z + 90 * side + xp)
        for side in range(2) for parity in range(2) for z in range(8) for xp in range(10)
    ]
    phase, octant = [], []
    for z in range(8):
        for y in range(8):
            for x in range(8):
                k = 4 * (z % 2) + 2 * (y % 2) + x % 2
                v = 16 * (z // 2) + 4 * (y // 2) + x // 2
                phase.append((128 * z + lane(y, x), 64 * k + v))
                k = 4 * (z // 4) + 2 * (y // 4) + x // 4
                v = 16 * (z % 4) + 4 * (y % 4) + x % 4
                octant.append((64 * k + v, 64 * z + 8 * y + x))
    flip = lambda pairs: [(b, a) for a, b in pairs]
    return (
        one_hot((128, 256), wrap),
        one_hot((128, 128), rewrap),
        one_hot((256, 128), native),
        one_hot((1024, 128), pack),
        one_hot((256, 2048), unpack),
        one_hot((1024, 512), phase),
        one_hot((512, 1024), flip(phase)),
        one_hot((512, 512), octant),
        one_hot((512, 512), flip(octant)),
    )


def dot(a, b):
    return jnp.dot(a, b, preferred_element_type=F32)


def dot_nt(a, b):
    return lax.dot_general(a, b, (((1,), (1,)), ((), ())), preferred_element_type=F32)


def roll(x, shift):
    return pltpu.roll(x, shift % 128, x.ndim - 1)


PERMUTATIONS = ("wrap", "rewrap", "native", "pack", "unpack", "phase", "unphase", "oct", "unoct")


def body(scale, *refs):
    operands, results, scratch = refs[:16], refs[16:20], refs[20:]
    nbr_h, occ_h, feat_h, dest_h, w_sub_h, w_down_h, cgrad = operands[:7]
    coarse, feat_grad, ws_out, wd_out = results
    nbr, occ, feat, dest_v, dest_s, w_sub, w_down = scratch[:7]
    p_wrap, p_rewrap, p_native, p_pack, p_unpack, p_phase, p_unphase, p_oct, p_unoct = scratch[7:16]
    (
        bank1, bank2, ysend, ydst, zsend, dsend, drecv, idx_v, idx_s, inv_v, inv_s, dest_buf, dest_in,
        cg_bank, og_in, og_all, og, ag_ph, ag, occ_p, r0, r1, act, phases, pg, wf, wb, wd, wdt,
        bl, bl_in, bl_bank, fg, wg, coarse_v, feat_v, ws_v,
        src, rc, s1, t1, t2, t3, fin, wd_v,
        h_send, h_recv, c_send, c_recv, in_sem, idx_sem, out_sem, r_send, r_recv,
    ) = scratch[16:]
    gz, gy = lax.axis_index("gz"), lax.axis_index("gy")
    cy, cz, core = gz // 8, (gz // 2) % 4, gz % 2
    nz, ny = 32, 4

    def at(dz, dy):
        return {"gz": (gz + dz + nz) % nz, "gy": (gy + dy + ny) % ny}

    def along(axis, d):
        if axis == 0:
            return {"gz": gz, "gy": (gy + d) % 4}
        if axis == 1:
            return {"gz": ((cy + d) % 4 * 4 + cz) * 2 + core, "gy": gy}
        return {"gz": (cy * 4 + (cz + d) % 4) * 2 + core, "gy": gy}

    coordinate = (gy, cy, cz)
    partner = {"gz": gz + 1 - 2 * core, "gy": gy}
    halo_steps = [(dz, dy) for dz in (-1, 0, 1) for dy in (-1, 0, 1) if (dz, dy) != (0, 0)]
    barrier = pltpu.get_barrier_semaphore()
    greeted = [at(*s) for s in halo_steps] + [partner]
    greeted += [along(axis, d) for axis in range(3) for d in (1, 2, 3)]
    for device in greeted:
        pl.semaphore_signal(barrier, inc=1, device_id=device, device_id_type=MESH)

    loads = {}

    def load(name, source, target):
        loads[name] = pltpu.make_async_copy(source, target, in_sem.at[len(loads)])
        loads[name].start()

    permuting = dict(zip(PERMUTATIONS, zip(operands[7:], scratch[7:16])))
    load("feat", feat_h, feat)
    load("occ", occ_h, occ)
    load("wrap", *permuting["wrap"])
    load("nbr", nbr_h, nbr)
    load("dest", dest_h, dest_v)
    load("dest_s", dest_h, dest_s)
    load("pack", *permuting["pack"])
    load("w_sub", w_sub_h, w_sub)
    load("w_down", w_down_h, w_down)
    load("cgrad", cgrad, cg_bank.at[pl.ds(0, 8)])
    for name in ("unoct", "unphase", "unpack", "rewrap", "phase", "native", "oct"):
        load(name, *permuting[name])

    def send(src, dst, send_sem, recv_sem, device):
        copy = pltpu.make_async_remote_copy(
            src_ref=src, dst_ref=dst, send_sem=send_sem, recv_sem=recv_sem,
            device_id=device, device_id_type=MESH,
        )
        copy.start()
        return copy

    lanes = lax.broadcasted_iota(jnp.int32, (64, 128), 1)
    low_half = lax.broadcasted_iota(jnp.int32, (128, 128), 1) < 64
    xp = lanes - 10 * lax.shift_right_logical(lanes * 205, 11)
    first, last = xp == 0, xp == 9
    low64 = lanes < 64
    yp_low, yp_high = lanes < 10, lanes >= 90
    center_row = lax.broadcasted_iota(jnp.int32, (8, 128), 1)
    center_x = center_row - 10 * lax.shift_right_logical(center_row * 205, 11)
    center = (center_row > 10) & (center_row < 89) & (center_x > 0) & (center_x < 9)

    loads["nbr"].wait()
    table = nbr[...]
    owner = table // 8
    slot = table - owner * 8
    step_z = owner // 4 - gz
    step_y = owner - owner // 4 * 4 - gy
    column = lax.broadcasted_iota(jnp.int32, (8, 27), 1)
    part_a = column // 9
    edge_z = jnp.where(part_a == 0, 7, 0)
    on_z = Z_LOW + jnp.where(step_z > 0, 8, 0) + slot
    on_diagonal = DIAGONAL + jnp.where(step_z > 0, 8, 0) + slot
    same_z = jnp.where(step_y == 0, 0, Y_SIDES) + slot * 8 + edge_z
    index = jnp.where(step_z == 0, same_z, jnp.where(step_y == 0, on_z, on_diagonal))
    index = jnp.where((table < 0) | ((part_a == 1) & (index > ZERO)), ZERO, index)
    idx_v[...] = jnp.zeros_like(idx_v)
    idx_v[:, 0:27] = index
    idx_copy = pltpu.make_async_copy(idx_v, idx_s, idx_sem.at[0])
    idx_copy.start()

    loads["feat"].wait()
    loads["occ"].wait()
    loads["wrap"].wait()
    for q in range(4):
        part = feat[:, :, 128 * q:128 * q + 128]
        flag = occ[:, 128 * q:128 * q + 128].astype(F32).astype(BF)
        rows = [part[t] * flag[t:t + 1] for t in range(8)]
        planes = dot(jnp.concatenate(rows, axis=0), p_wrap[...]).astype(BF)
        flags = dot(flag, p_wrap[...])
        for h in range(2):
            flag_plane = jnp.where(center, flags[:, 128 * h:128 * h + 128], 0.0)
            for t in range(8):
                occ_p[t, :, 128 * (2 * q + h):128 * (2 * q + h) + 128] = flag_plane[t:t + 1]
                bank1[8 * t + 2 * q + h] = planes[64 * t:64 * t + 64, 128 * h:128 * h + 128]

    loads["dest"].wait()
    dest_buf[0] = jnp.zeros((8, 128), jnp.int32) - 1
    dest_buf[0, 0:1, 0:8] = dest_v[...]
    for bank in (bank1, bank2):
        bank[ZERO:ZERO + 8] = jnp.zeros((8, 64, 128), BF)
    loads["pack"].wait()

    pl.semaphore_wait(barrier, len(greeted))
    dest_send = send(dest_buf.at[0], dest_buf.at[1], c_send.at[0], c_recv.at[0], partner)
    cg_send = send(cgrad, cg_bank.at[pl.ds(8, 8)], c_send.at[1], c_recv.at[1], partner)

    def publish(bank, which):
        copies = []
        total = None
        for q in range(4):
            both = jnp.concatenate(
                [
                    jnp.concatenate([bank[8 * t + 2 * q], bank[8 * t + 2 * q + 1]], axis=1)
                    for t in range(8)
                ],
                axis=0,
            )
            term = dot(both, p_pack[256 * q:256 * q + 256, :])
            total = term if total is None else total + term
        for j in range(4):
            even, odd = total[128 * j:128 * j + 64], total[128 * j + 64:128 * j + 128]
            ysend[which, 0, j] = jnp.where(low64, even, roll(odd, 64)).astype(BF)
            ysend[which, 1, j] = jnp.where(low64, roll(even, 64), odd).astype(BF)
        for side in range(2):
            for t in range(8):
                zsend[which, side, t] = bank[8 * t + (7 if side == 0 else 0)]
        for side in range(2):
            up = 1 - 2 * side
            copies.append(
                send(
                    ysend.at[which, side], ydst.at[which, side],
                    h_send.at[which, side], h_recv.at[which, side], at(0, up),
                )
            )
            copies.append(
                send(
                    zsend.at[which, side], bank.at[pl.ds(Z_LOW if side == 0 else Z_HIGH, 8)],
                    h_send.at[which, 2 + side], h_recv.at[which, 2 + side], at(up, 0),
                )
            )
        for side_z in range(2):
            for side_y in range(2):
                number = 2 * side_z + side_y
                gathered = None
                for t in range(8):
                    piece = bank[8 * t + (7 if side_z == 0 else 0)].astype(F32)
                    piece = roll(piece, 16 * t - 90 * side_y)
                    piece = jnp.where((lanes >= 16 * t) & (lanes < 16 * t + 10), piece, 0.0)
                    gathered = piece if gathered is None else gathered + piece
                dsend[which, number] = gathered.astype(BF)
                copies.append(
                    send(
                        dsend.at[which, number], drecv.at[which, number],
                        h_send.at[which, 4 + number], h_recv.at[which, 4 + number],
                        at(1 - 2 * side_z, 1 - 2 * side_y),
                    )
                )
        return copies

    def receive(bank, which, copies):
        for copy in copies:
            copy.wait_recv()
        rows = jnp.concatenate([ydst[which, side].reshape(256, 128) for side in range(2)], axis=1)
        for q in range(8):
            planes = dot(rows, p_unpack[:, 256 * q:256 * q + 256]).astype(BF)
            for j in range(4):
                for h in range(2):
                    t, z = 2 * j + q // 4, 2 * (q % 4) + h
                    bank[Y_SIDES + 8 * t + z] = planes[64 * j:64 * j + 64, 128 * h:128 * h + 128]
        for side_z in range(2):
            below = drecv[which, 2 * side_z].astype(F32)
            above = drecv[which, 2 * side_z + 1].astype(F32)
            for t in range(8):
                bank[DIAGONAL + 8 * side_z + t] = jnp.where(
                    yp_low, roll(below, -16 * t), roll(above, 90 - 16 * t)
                ).astype(BF)

    def assemble(bank, t, r_buf, i, planes):
        for zp in planes:
            a = 0 if zp == 0 else (2 if zp == 9 else 1)
            rows = []
            for b in range(3):
                loaded = []
                for c in range(3):
                    place = idx_s[t, 9 * a + 3 * b + c] + (zp - 1 if a == 1 else 0)
                    loaded.append(bank[place])
                rows.append(jnp.where(first, loaded[0], jnp.where(last, loaded[2], loaded[1])))
            plane = jnp.where(yp_low, rows[0], jnp.where(yp_high, rows[2], rows[1]))
            columns = slice(128 * zp, 128 * zp + 128)
            r_buf[i, 0:64, columns] = roll(plane, 10)
            r_buf[i, 64:128, columns] = plane
            r_buf[i, 128:192, columns] = roll(plane, -10)

    def convolve(weights, r_buf, i, q):
        total = None
        for a in range(3):
            term = dot(weights[a], r_buf[i, :, 128 * a + 256 * q:128 * a + 256 * q + 256])
            total = term if total is None else total + term
        parts = []
        for h in range(2):
            y = total[:, 128 * h:128 * h + 128]
            parts.append(roll(y[0:64], 1) + y[64:128] + roll(y[128:192], -1))
        return parts

    groups = ((0, 1, 2), (3, 4, 5), (6, 7), (8, 9))

    def sweep(bank, low, high, tile):
        if low == 0:
            for planes in groups:
                assemble(bank, 0, r0, 0, planes)

        @pl.loop(low, high)
        def _(i):
            for q in range(4):
                assemble(bank, 2 * i + 1, r1, i, groups[q])
                tile(r0, i, 2 * i, q)
            for q in range(4):
                assemble(bank, jnp.minimum(2 * i + 2, 7), r0, i + 1, groups[q])
                tile(r1, i, 2 * i + 1, q)

    halo = publish(bank1, 0)

    loads["w_sub"].wait()
    loads["w_down"].wait()
    for a in range(3):
        for c in range(3):
            wf[a, 64 * c:64 * c + 64, :] = jnp.concatenate(
                [w_sub[9 * a + 3 * b + c].astype(F32) for b in range(3)], axis=1
            ).astype(BF)
        turned = jnp.concatenate(
            [
                jnp.concatenate(
                    [w_sub[9 * (2 - a) + 3 * (2 - b) + 2 - c].astype(F32) for c in range(3)], axis=1
                )
                for b in range(3)
            ],
            axis=0,
        )
        wb[a] = turned.T.astype(BF)
    wdt[...] = w_down[...].reshape(512, 128)
    wd[...] = wdt[...].astype(F32).T.astype(BF)

    cg_bank[16] = jnp.zeros((128, 512), BF)
    idx_copy.wait()
    loads["dest_s"].wait()
    loads["cgrad"].wait()
    loads["unoct"].wait()
    cg_send.wait_recv()
    base = gz * 4 + gy
    partner_index = (gz + 1 - 2 * core) * 4 + gy
    for t in range(8):
        d = dest_s[0, t]
        own = d // 8 - base * 8
        other = d // 8 - partner_index * 8
        chosen = jnp.where((other >= 0) & (other < 8), 8 + other, 16)
        chosen = jnp.where((own >= 0) & (own < 8), own, chosen)
        og_in[128 * t:128 * t + 128, :] = cg_bank[chosen]
    for q in range(2):
        split = dot(og_in[...], p_unoct[:, 256 * q:256 * q + 256]).astype(BF)
        for t in range(8):
            for h in range(2):
                og_all[4 * t + 2 * q + h] = split[128 * t:128 * t + 128, 128 * h:128 * h + 128]
    for j in range(4):
        halves = []
        for h in range(2):
            t = 2 * j + h
            d = dest_s[0, t]
            octant = d - d // 8 * 8
            piece = og_all[4 * t + octant // 2].astype(F32)
            odd = octant - octant // 2 * 2
            halves.append(jnp.where(odd == h, piece, roll(piece, 64)))
        og[:, 128 * j:128 * j + 128] = jnp.where(low_half, halves[0], halves[1]).astype(BF)
    for r in range(4):
        rows = dot(wdt[128 * r:128 * r + 128, :], og[...]).astype(BF).astype(F32)
        for j in range(4):
            even = rows[0:64, 128 * j:128 * j + 128]
            odd = rows[64:128, 128 * j:128 * j + 128]
            columns = slice(128 * r, 128 * r + 128)
            ag_ph[128 * j:128 * j + 64, columns] = jnp.where(low64, even, roll(odd, 64)).astype(BF)
            ag_ph[128 * j + 64:128 * j + 128, columns] = jnp.where(
                low64, roll(even, 64), odd
            ).astype(BF)
    loads["unphase"].wait()
    for q in range(4):
        spread = dot(ag_ph[...], p_unphase[:, 256 * q:256 * q + 256]).astype(BF)
        for t in range(8):
            ag[t, :, 256 * q:256 * q + 256] = spread[64 * t:64 * t + 64]

    dest_send.wait_recv()
    dest_copy = pltpu.make_async_copy(dest_buf.at[1], dest_in, idx_sem.at[2])
    dest_copy.start()
    dest_copy.wait()
    place = lax.broadcasted_iota(jnp.int32, (8, 128), 1) + base * 64
    inverse = jnp.zeros((8, 128), jnp.int32) + 16
    for s in range(8):
        inverse = jnp.where(place == dest_s[0, s], s, inverse)
        inverse = jnp.where(place == dest_in[0, s], 8 + s, inverse)
    inv_v[...] = inverse
    inv_copy = pltpu.make_async_copy(inv_v, inv_s, idx_sem.at[3])
    inv_copy.start()

    loads["unpack"].wait()
    receive(bank1, 0, halo)

    def forward(r_buf, i, t, q):
        parts = convolve(wf, r_buf, i, q)
        for h in range(2):
            z = 2 * q + h
            v = parts[h]
            on = occ_p[t, :, 128 * z:128 * z + 128]
            s = 1.0 / (1.0 + jnp.exp(-v))
            act[t, :, 128 * z:128 * z + 128] = jnp.where(on > 0.5, v * s, 0.0).astype(BF)
            g = ag[t, :, 128 * z:128 * z + 128].astype(F32)
            g = g * s * (1.0 + v * (1.0 - s))
            pg[8 * t + z] = jnp.where(on > 0.5, g, 0.0).astype(BF)

    sweep(bank1, 0, 4, forward)

    wg[...] = jnp.zeros_like(wg)

    @pl.loop(0, 4)
    def _(i):
        for h in range(2):
            planes = [pg[8 * (2 * i + h) + z] for z in range(8)]
            shifted = jnp.concatenate(
                [
                    jnp.concatenate([roll(p, c - 1) for p in planes], axis=1)
                    for c in range(3)
                ],
                axis=0,
            )
            for a in range(3):
                wg[a] += dot_nt(shifted, (r0, r1)[h][i, :, 128 * a:128 * a + 1024])

    for a in range(3):
        src[192 * a:192 * a + 192, :] = wg[a, :, 0:128]
    src[576:768, :] = jnp.concatenate([wg[0, :, 128:192], wg[1, :, 128:192]], axis=1)
    src[768:960, 0:64] = wg[2, :, 128:192]
    src[768:960, 64:128] = jnp.zeros((192, 64), F32)
    src[960:1024, :] = jnp.zeros((64, 128), F32)


    def pair(n):
        return r_send.at[n], r_recv.at[n]

    def rows_at(start, size):
        return pl.ds(pl.multiple_of(start, 8), size)

    def axis_of(p, stage):
        return (p + stage) % 3

    def me(p, stage):
        return coordinate[axis_of(p, stage)]

    def first_row(p, half):
        return 512 * half + 256 * p if p < 2 else 1024 + 256 * half

    def stage_0(p, _):
        rows = rows_at(first_row(p, 1 - core), 256)
        return [send(src.at[rows], rc.at[p], *pair(p), partner)]

    def arrived(copies):
        for copy in copies:
            copy.wait_recv()

    def stage_1(p, before):
        arrived(before)
        s1[p] = src[rows_at(first_row(p, core), 256)] + rc[p]
        copies = []
        for d in (1, 2, 3):
            to = (me(p, 0) + d) % 4
            copies.append(
                send(
                    s1.at[p, rows_at(64 * to, 64)], t1.at[p, d - 1],
                    *pair(3 + 3 * p + d - 1), along(axis_of(p, 0), d),
                )
            )
        return copies

    def exchange(buffer, p, stage, value, first_pair):
        buffer[p, me(p, stage)] = value
        place = buffer.at[p, me(p, stage)]
        return [
            send(place, place, *pair(first_pair + 3 * p + d - 1), along(axis_of(p, stage), d))
            for d in (1, 2, 3)
        ]

    def stage_2(p, before):
        arrived(before)
        total = s1[p, rows_at(64 * me(p, 0), 64)]
        for d in range(3):
            total = total + t1[p, d]
        return exchange(t2, p, 1, total, 12)

    def stage_3(p, before):
        arrived(before)
        return exchange(t3, p, 2, (t2[p, 0] + t2[p, 1]) + (t2[p, 2] + t2[p, 3]), 21)

    def stage_4(p, before):
        arrived(before)
        rows = rows_at(first_row(p, core) + 64 * me(p, 0), 64)
        total = (t3[p, 0] + t3[p, 1]) + (t3[p, 2] + t3[p, 3])
        fin[rows] = (total * scale).astype(BF)
        return [
            send(fin.at[rows], fin.at[rows], *pair(30 + 3 * p + d - 1), along(axis_of(p, 0), d))
            for d in (1, 2, 3)
        ]

    def stage_5(p, before):
        arrived(before)
        rows = rows_at(first_row(p, core), 256)
        return [send(fin.at[rows], fin.at[rows], *pair(39 + p), partner)]

    stages = [stage_0, stage_1, stage_2, stage_3, stage_4, stage_5]
    reduced = [[], [], []]

    def reduce_step(*parts):
        for p in parts:
            n = len(reduced[p])
            reduced[p].append(stages[n](p, reduced[p][-1] if n > 0 else None))

    loads["phase"].wait()
    for q in range(2):
        split = dot(act[...].reshape(512, 1024), p_phase[:, 256 * q:256 * q + 256])
        for j in range(4):
            for h in range(2):
                even = split[128 * j:128 * j + 64, 128 * h:128 * h + 128]
                odd = split[128 * j + 64:128 * j + 128, 128 * h:128 * h + 128]
                k = 4 * q + 2 * h
                columns = slice(128 * j, 128 * j + 128)
                phases[64 * k:64 * k + 64, columns] = jnp.where(
                    low64, even, roll(odd, 64)
                ).astype(BF)
                phases[64 * k + 64:64 * k + 128, columns] = jnp.where(
                    low64, roll(even, 64), odd
                ).astype(BF)
    src[1024:1536, :] = dot_nt(phases[...], og[...])

    reduce_step(0, 1, 2)
    bl[...] = dot(wd[...], phases[...]).astype(BF)
    bl_send = send(bl, bl_in, c_send.at[2], c_recv.at[2], partner)

    loads["rewrap"].wait()
    for t in range(8):
        rows = pg[8 * t:8 * t + 8].reshape(512, 128)
        bank2[8 * t:8 * t + 8] = dot(rows, p_rewrap[...]).astype(BF).reshape(8, 64, 128)

    reduce_step(0, 1, 2)
    halo2 = publish(bank2, 1)

    inv_copy.wait()
    bl_send.wait_recv()
    bl_bank[16] = jnp.zeros((128, 128), BF)
    for source in range(2):
        blocks = (bl, bl_in)[source]
        for j in range(4):
            both = blocks[:, 128 * j:128 * j + 128].astype(F32)
            turned = roll(both, 64)
            bl_bank[8 * source + 2 * j] = jnp.where(low_half, both, turned).astype(BF)
            bl_bank[8 * source + 2 * j + 1] = jnp.where(low_half, turned, both).astype(BF)
    for c in range(8):
        for q in range(4):
            even = bl_bank[inv_s[0, 8 * c + 2 * q]]
            odd = bl_bank[inv_s[0, 8 * c + 2 * q + 1]]
            og_in[128 * c:128 * c + 128, 128 * q:128 * q + 128] = jnp.where(low_half, even, odd)
    loads["oct"].wait()
    for q in range(2):
        rows = dot(og_in[...], p_oct[:, 256 * q:256 * q + 256]).astype(BF)
        coarse_v[:, :, 256 * q:256 * q + 256] = rows.reshape(8, 128, 256)
    coarse_out = pltpu.make_async_copy(coarse_v, coarse, out_sem.at[1])
    coarse_out.start()
    reduce_step(0, 1, 2)
    receive(bank2, 1, halo2)
    reduce_step(0, 1, 2)

    def backward(r_buf, i, t, q):
        parts = convolve(wb, r_buf, i, q)
        for h in range(2):
            z = 2 * q + h
            on = occ_p[t, :, 128 * z:128 * z + 128]
            fg[t, :, 128 * z:128 * z + 128] = jnp.where(on > 0.5, parts[h], 0.0).astype(BF)

    sweep(bank2, 0, 2, backward)
    reduce_step(0, 1, 2)
    sweep(bank2, 2, 4, backward)
    reduce_step(0, 1, 2)
    loads["native"].wait()
    for q in range(4):
        rows = dot(fg[:, :, 256 * q:256 * q + 256].reshape(512, 256), p_native[...])
        feat_v[:, :, 128 * q:128 * q + 128] = rows.astype(BF).reshape(8, 64, 128)
    feat_out = pltpu.make_async_copy(feat_v, feat_grad, out_sem.at[0])
    feat_out.start()

    arrived(reduced[0][5] + reduced[1][5])
    for a in range(3):
        for c in range(3):
            for b in range(2):
                rows = slice(192 * a + 64 * c, 192 * a + 64 * c + 64)
                ws_v[9 * a + 3 * b + c] = fin[rows, 64 * b:64 * b + 64].astype(F32)
            row, column = ((576, 0), (576, 64), (768, 0))[a]
            rows = slice(row + 64 * c, row + 64 * c + 64)
            ws_v[9 * a + 6 + c] = fin[rows, column:column + 64].astype(F32)
    sub_out = pltpu.make_async_copy(ws_v, ws_out, out_sem.at[3])
    sub_out.start()
    arrived(reduced[2][5])
    wd_v[...] = fin[1024:1536, :].astype(F32)
    down_out = pltpu.make_async_copy(wd_v, wd_out, out_sem.at[2])
    down_out.start()
    for copy in halo + halo2 + [dest_send, cg_send, bl_send]:
        copy.wait_send()
    for stage in reduced:
        for copies in stage:
            for copy in copies:
                copy.wait_send()
    for copy in (feat_out, coarse_out, down_out, sub_out):
        copy.wait()


def write_out(*refs):
    sources, targets, sems = refs[:4], refs[4:8], refs[8]
    copies = [pltpu.make_async_copy(a, b, sems.at[n]) for n, (a, b) in enumerate(zip(sources, targets))]
    for copy in copies:
        copy.start()
    for copy in copies:
        copy.wait()


def shards(features, occupancy, neighbors, coarse_dest, w_sub, w_down, coarse_grad):
    devices = lax.axis_size("gz") * lax.axis_size("gy")
    scale = (features.shape[0] * devices * 512.0) ** -0.5
    anywhere = pl.BlockSpec(memory_space=pl.ANY)
    constants = permutations()
    vmem, smem, dma = pltpu.VMEM, pltpu.SMEM, pltpu.SemaphoreType.DMA
    i32 = jnp.int32
    held = pl.pallas_call(
        functools.partial(body, scale),
        out_shape=(
            vmem((8, 128, 512), BF), vmem((8, 64, 512), BF), vmem((27, 64, 64), F32), vmem((512, 128), F32),
        ),
        in_specs=[anywhere] * 16,
        out_specs=(anywhere,) * 4,
        scratch_shapes=[
            vmem((8, 27), i32), vmem((8, 512), i32), vmem((8, 64, 512), BF), vmem((1, 8), i32),
            smem((1, 8), i32), vmem((27, 64, 64), BF), vmem((8, 64, 128), BF),
        ] + [vmem(c.shape, BF) for c in constants] + [
            vmem((BANK, 64, 128), BF), vmem((BANK, 64, 128), BF),
            vmem((2, 2, 4, 64, 128), BF), vmem((2, 2, 4, 64, 128), BF), vmem((2, 2, 8, 64, 128), BF),
            vmem((2, 4, 64, 128), BF), vmem((2, 4, 64, 128), BF),
            vmem((8, 128), i32), smem((8, 128), i32), vmem((8, 128), i32), smem((8, 128), i32),
            vmem((2, 8, 128), i32), smem((8, 128), i32),
            vmem((17, 128, 512), BF), vmem((1024, 512), BF), vmem((32, 128, 128), BF),
            vmem((128, 512), BF), vmem((512, 512), BF), vmem((8, 64, 1024), BF),
            vmem((8, 1, 1024), F32), vmem((5, 192, 1280), BF), vmem((4, 192, 1280), BF),
            vmem((8, 64, 1024), BF), vmem((512, 512), BF), vmem((64, 64, 128), BF),
            vmem((3, 192, 192), BF), vmem((3, 192, 192), BF), vmem((128, 512), BF), vmem((512, 128), BF),
            vmem((128, 512), BF), vmem((128, 512), BF), vmem((17, 128, 128), BF),
            vmem((8, 64, 1024), BF), vmem((3, 192, 192), F32),
            vmem((8, 128, 512), BF), vmem((8, 64, 512), BF), vmem((27, 64, 64), F32),
            vmem((1536, 128), F32), vmem((3, 256, 128), F32), vmem((3, 256, 128), F32),
            vmem((3, 3, 64, 128), F32), vmem((3, 4, 64, 128), F32), vmem((3, 4, 64, 128), F32),
            vmem((1536, 128), BF), vmem((512, 128), F32),
            dma((2, 8)), dma((2, 8)), dma((3,)), dma((3,)), dma((18,)), dma((4,)), dma((4,)),
            dma((42,)), dma((42,)),
        ],
        compiler_params=pltpu.CompilerParams(
            collective_id=0, has_side_effects=True, vmem_limit_bytes=60 * 1024 * 1024
        ),
        cost_estimate=pl.CostEstimate(flops=6 * 10**9, bytes_accessed=12 * 10**6, transcendentals=10**6),
        name="sparse_conv",
    )(
        neighbors, occupancy, features, coarse_dest.reshape(1, 8), w_sub,
        w_down.transpose(0, 2, 1), coarse_grad, *constants,
    )
    coarse, feat_grad, ws, wd = pl.pallas_call(
        write_out,
        out_shape=[jax.ShapeDtypeStruct(x.shape, x.dtype) for x in held],
        in_specs=[anywhere] * 4,
        out_specs=[anywhere] * 4,
        scratch_shapes=[dma((4,))],
        compiler_params=pltpu.CompilerParams(vmem_limit_bytes=1024 * 1024),
        name="write_out",
    )(*held)
    return coarse, feat_grad, ws, wd.reshape(8, 64, 128).transpose(0, 2, 1)


def solution(mesh):
    return jax.shard_map(
        shards,
        mesh=mesh,
        in_specs=(
            P(("gz", "gy"), None, None),
            P(("gz", "gy"), None),
            P(("gz", "gy"), None),
            P(("gz", "gy")),
            P(),
            P(),
            P(("gz", "gy"), None, None),
        ),
        out_specs=(P(("gz", "gy"), None, None), P(("gz", "gy"), None, None), P(), P()),
        check_vma=False,
    )
```
